512 devices in a mesh: tm: 16 (over y, core), space: 32 (over x, z).
Axes of the slice: x: 4, y: 8, z: 8, core: 2. Of those that a mesh axis runs over, the one named last changes fastest.
Arguments:
- initial: float32 [16, 128, 32768], P('tm', None, 'space'), may hold values from -324 to 324
- rhs: float32 [16, 128, 32768], P('tm', None, 'space'), may hold values from -324 to 324
- coef: float32 [32768], P('space'), may hold values from 0.5 to 4
- stiffness: float32 [128, 128], replicated, may hold values from -0.5 to 0.5
- block_inverse: float32 [128, 128], replicated, may hold values from -0.5 to 0.5
- face_proj: float32 [192, 128], replicated, may hold values from -0.5 to 0.5
- lift: float32 [128, 192], replicated, may hold values from -0.4375 to 0.4375
- time_lift: float32 [128, 64], replicated, may hold values from -0.75 to 0.75
- neighbour: int32 [6, 32768], P(None, 'space'), may hold values from 0 to 6399, as said below
- boundary: int32 [6, 32768], P(None, 'space'), may hold values from 0 to 1, as said below
- send_list: int32 [8192], P('space'), may hold values from 0 to 2047, as said below
Outputs:
- smoothed: float32 [16, 128, 32768], P('tm', None, 'space')
- indicator: float32 [16, 32768], P('tm', 'space')
- estimate: float32 [1], replicated
The draws below stay inside these ranges and needn't reach their ends.
Inputs may be any that keep to these rules, and one draw needn't show every extreme that they name: `neighbour`: the elements form a structured hexahedral grid numbered in a random order inside each partition; partition p holds 8 element layers and meets partitions p - 1 and p + 1 across 128 faces each, listed in the same order on both sides. Interior faces point to the opposite face of the neighbouring element; faces toward another partition point to columns 6144 and above; boundary faces may point anywhere. `boundary`: marks the outer faces of the whole grid. `send_list`: the first 128 entries of a partition list its faces facing the lower partition, the next 128 those facing the upper one, as columns of its own pool below 2048.
All inputs are finite; a program needn't handle non-finite values.
Results may differ from the reference program's by a relative error of at most 0.000059.
Values sent between devices are 32-bit elements; how exact they have to be, the bound alone decides.
A program may use at most 64 MiB of HBM per device.

```python
import math
import jax
import jax.numpy as jnp
from jax import lax

DOFS = 128
SDOFS = 64
FDOFS = 32
GX = 8
GY = 8
GZ = 16
E_DEV = 1024
NB = 128
ELEMS = 32768
SLABS = 16


def slot_order(sub_key):
    middle = 1 + jax.random.permutation(sub_key, E_DEV - 2)
    return jnp.concatenate([jnp.zeros((1,), jnp.int32), middle.astype(jnp.int32), jnp.full((1,), E_DEV - 1, jnp.int32)])


def mesh_tables(key):
    partitions = ELEMS // E_DEV
    layer_size = GY * GZ
    slot_keys = jax.random.split(jax.random.fold_in(key, 101), partitions)
    slot_of = jax.vmap(slot_order)(slot_keys).astype(jnp.int32)
    cell_ids = jnp.arange(E_DEV, dtype=jnp.int32)
    coord_x = cell_ids // layer_size
    coord_y = cell_ids // GZ % GY
    coord_z = cell_ids % GZ
    lateral = cell_ids % layer_size
    part_ids = jnp.arange(partitions, dtype=jnp.int32)[:, None]
    columns = []
    walls = []
    for face_id in range(6):
        direction = face_id // 2
        offset = 2 * (face_id % 2) - 1
        next_x = coord_x + (offset if direction == 0 else 0)
        next_y = coord_y + (offset if direction == 1 else 0)
        next_z = coord_z + (offset if direction == 2 else 0)
        inside = (next_x >= 0) & (next_x < GX) & (next_y >= 0) & (next_y < GY) & (next_z >= 0) & (next_z < GZ)
        next_cell = (jnp.clip(next_x, 0, GX - 1) * GY + jnp.clip(next_y, 0, GY - 1)) * GZ + jnp.clip(next_z, 0, GZ - 1)
        local_col = (face_id ^ 1) * E_DEV + slot_of[:, next_cell]
        if direction == 0:
            remote = 6 * E_DEV + face_id % 2 * layer_size + lateral
            column = jnp.where(inside[None, :], local_col, remote[None, :])
            end_part = 0 if face_id == 0 else partitions - 1
            is_wall = jnp.logical_not(inside)[None, :] & (part_ids == end_part)
        else:
            column = jnp.where(inside[None, :], local_col, 0)
            is_wall = jnp.broadcast_to(jnp.logical_not(inside)[None, :], (partitions, E_DEV))
        columns.append(column.astype(jnp.int32))
        walls.append(is_wall.astype(jnp.int32))

    def place(values_row, slot_row):
        return jnp.zeros_like(values_row).at[:, slot_row].set(values_row)
    placed_cols = jax.vmap(place)(jnp.stack(columns, axis=1), slot_of)
    placed_walls = jax.vmap(place)(jnp.stack(walls, axis=1), slot_of)
    neighbour = placed_cols.transpose(1, 0, 2).reshape(6, ELEMS)
    boundary = placed_walls.transpose(1, 0, 2).reshape(6, ELEMS)
    lower_list = slot_of[:, :layer_size]
    upper_list = E_DEV + slot_of[:, (GX - 1) * layer_size:]
    send_list = jnp.concatenate([lower_list, upper_list], axis=1).reshape(2 * layer_size * partitions)
    return (neighbour.astype(jnp.int32), boundary.astype(jnp.int32), send_list.astype(jnp.int32))


def draw_neighbour(key, part):
    return mesh_tables(key)[0]


def draw_boundary(key, part):
    return mesh_tables(key)[1]


def draw_send_list(key, part):
    return mesh_tables(key)[2]


def ramped(key, salt):
    sub_key = jax.random.fold_in(key, salt)
    shape_all = (SLABS, DOFS, ELEMS)
    growth = 3.0
    noise_draw = jax.random.truncated_normal(sub_key, -4.0, 4.0, shape_all, jnp.float32)
    slab_pos = jnp.arange(SLABS, dtype=jnp.float32)[:, None, None] / max(SLABS - 1, 1)
    part_pos = (jnp.arange(ELEMS) // E_DEV).astype(jnp.float32)[None, None, :] / max(ELEMS // E_DEV - 1, 1)
    return noise_draw * growth ** slab_pos * growth ** part_pos


def draw_initial(key, part):
    return ramped(key, 11)


def draw_rhs(key, part):
    return ramped(key, 23)


def steps_of(stream_key, shape, pieces, low, largest):
    def one(dim, parts):
        heights = jax.random.uniform(jax.random.fold_in(jax.random.fold_in(stream_key, 6), dim), (parts,), jnp.float32, low / len(pieces), largest / len(pieces))
        return jnp.repeat(jnp.exp(heights), shape[dim] // parts).reshape((-1,) + (1,) * (len(shape) - dim - 1))

    factor_of = one(*pieces[0])
    for cut in pieces[1:]:
        factor_of = factor_of * one(*cut)
    return factor_of


def normal_values(key, dims, scale, most, kind=jnp.bfloat16):
    values = scale * jax.random.normal(key, dims, jnp.float32)
    return jnp.clip(values, min=-most, max=most).astype(kind)


def setup_inputs(seed: int = 0) -> dict:
    keys = jax.random.split(jax.random.key(seed), 12)
    initial = draw_initial(jax.random.fold_in(keys[11], 71), 0)
    rhs = draw_rhs(jax.random.fold_in(keys[11], 71), 0)
    coef = jnp.clip(jnp.exp(math.log(4.0) - 2.0794415 * jax.random.uniform(keys[2], (ELEMS,), jnp.float32) ** steps_of(keys[2], (ELEMS,), ((0, 32),), -0.2, 0.2)), 0.5, 4.0)
    stiffness = normal_values(keys[3], (DOFS, DOFS), DOFS ** -0.5, 0.5, jnp.float32)
    block_inverse = normal_values(keys[4], (DOFS, DOFS), DOFS ** -0.5, 0.5, jnp.float32)
    face_proj = normal_values(keys[5], (6 * FDOFS, DOFS), DOFS ** -0.5, 0.5, jnp.float32)
    lift = normal_values(keys[6], (DOFS, 6 * FDOFS), (6 * FDOFS) ** -0.5, 0.4375, jnp.float32)
    time_lift = normal_values(keys[7], (DOFS, SDOFS), SDOFS ** -0.5, 0.75, jnp.float32)
    neighbour = draw_neighbour(jax.random.fold_in(keys[11], 71), 0)
    boundary = draw_boundary(jax.random.fold_in(keys[11], 71), 0)
    send_list = draw_send_list(jax.random.fold_in(keys[11], 71), 0)
    return {"initial": initial, "rhs": rhs, "coef": coef, "stiffness": stiffness, "block_inverse": block_inverse, "face_proj": face_proj, "lift": lift, "time_lift": time_lift, "neighbour": neighbour, "boundary": boundary, "send_list": send_list}


def slab_terms(vector, prev_end, coef, stiffness, face_proj, lift, time_lift, neighbour, boundary, send_list):
    partitions = ELEMS // E_DEV
    half_dofs = vector.shape[0] // 2
    traces = jnp.dot(face_proj, vector, precision=lax.Precision.HIGHEST)
    face_dofs = traces.shape[0] // 6
    trace_pool = traces.reshape(face_dofs, 6, partitions, E_DEV).transpose(2, 0, 1, 3).reshape(partitions, face_dofs, 6 * E_DEV)
    send_ids = jnp.broadcast_to(send_list.reshape(partitions, 1, 2 * NB), (partitions, face_dofs, 2 * NB))
    outbound = jnp.take_along_axis(trace_pool, send_ids, axis=2)
    zero_rim = jnp.zeros((1, face_dofs, NB), jnp.float32)
    from_lower = jnp.concatenate([zero_rim, outbound[:-1, :, NB:]], axis=0)
    from_upper = jnp.concatenate([outbound[1:, :, :NB], zero_rim], axis=0)
    ext_pool = jnp.concatenate([trace_pool, from_lower, from_upper], axis=2)
    column_ids = neighbour.reshape(6, partitions, E_DEV).transpose(1, 0, 2).reshape(partitions, 1, 6 * E_DEV)
    column_ids = jnp.broadcast_to(column_ids, (partitions, face_dofs, 6 * E_DEV))
    outside = jnp.take_along_axis(ext_pool, column_ids, axis=2)
    outside = outside.reshape(partitions, face_dofs, 6, E_DEV).transpose(1, 2, 0, 3).reshape(face_dofs * 6, ELEMS)
    open_faces = jnp.tile(1.0 - boundary.astype(jnp.float32), (face_dofs, 1))
    face_jump = traces - outside * open_faces
    time_jump = vector[:half_dofs] - prev_end
    applied = coef * jnp.dot(stiffness, vector, precision=lax.Precision.HIGHEST)
    applied = applied + jnp.dot(lift, face_jump, precision=lax.Precision.HIGHEST)
    applied = applied + jnp.dot(time_lift, time_jump, precision=lax.Precision.HIGHEST)
    return (applied, lax.optimization_barrier(jnp.sum(face_jump * face_jump, axis=0)), lax.optimization_barrier(jnp.sum(time_jump * time_jump, axis=0)))

def apply_all(state, coef, stiffness, face_proj, lift, time_lift, neighbour, boundary, send_list):
    half_dofs = state.shape[1] // 2
    prev_ends = jnp.concatenate([jnp.zeros((1, half_dofs, state.shape[2]), jnp.float32), state[:-1, half_dofs:, :]], axis=0)

    def one_slab(pair):
        return slab_terms(pair[0], pair[1], coef, stiffness, face_proj, lift, time_lift, neighbour, boundary, send_list)
    return lax.map(one_slab, (state, prev_ends))

def reference(initial, rhs, coef, stiffness, block_inverse, face_proj, lift, time_lift, neighbour, boundary, send_list):
    operands = (coef, stiffness, face_proj, lift, time_lift, neighbour, boundary, send_list)
    applied_base, unused_face, unused_time = apply_all(initial, *operands)
    residual = rhs - applied_base
    direction = jnp.einsum('ik,ske->sie', block_inverse, residual, precision=lax.Precision.HIGHEST) / coef
    image, unused_face, unused_time = apply_all(direction, *operands)
    step_size = jnp.sum(residual * image) / jnp.sum(image * image)
    smoothed = initial + step_size * direction
    new_residual = residual - step_size * image
    unused_image, face_sq, time_sq = apply_all(smoothed, *operands)
    element_eta = lax.optimization_barrier(jnp.sum(new_residual * new_residual, axis=1)) + 0.5 * face_sq + time_sq
    eta_total = jnp.sum(element_eta)
    element_count = SLABS * ELEMS
    indicator = element_eta * element_count / eta_total
    estimate = jnp.sqrt(eta_total / element_count).reshape(1)
    return (smoothed, indicator, estimate)
```

```python
import functools

import jax
import jax.numpy as jnp
from jax import lax
from jax.experimental import pallas as pl
from jax.experimental.pallas import tpu as pltpu
from jax.sharding import PartitionSpec as P

MESH = pl.DeviceIdType.MESH
F32 = jnp.float32
BF16 = jnp.bfloat16
D = 128
H = 64
FD = 32
R = 192
LAYERS = 8
NB = 128
E = 1024


def split(x):
    high = x.astype(BF16)
    return high, (x - high.astype(F32)).astype(BF16)


def dot(a, b):
    return jnp.dot(a, b, preferred_element_type=F32)


def iota(shape, dim):
    return lax.broadcasted_iota(jnp.int32, shape, dim)


def one_hot(mask):
    return jnp.where(mask, 1.0, 0.0).astype(BF16)


def column(row):
    eye = iota((NB, NB), 0) == iota((NB, NB), 1)
    return jnp.sum(jnp.where(eye, jnp.broadcast_to(row, (NB, NB)), 0), axis=1, keepdims=True)


def lookup(table, index):
    lane = jnp.broadcast_to(index & 127, (8, NB))
    line = jnp.broadcast_to(index >> 7, (8, NB))
    found = jnp.take_along_axis(table, lane, axis=1)
    return jnp.sum(jnp.where(line == iota((8, NB), 0), found, 0), axis=0, keepdims=True)


def layer(k):
    return slice(k * NB, (k + 1) * NB)


def kernel(
    nt,
    ns,
    init_h,
    rhs_h,
    coef_h,
    stiff_h,
    binv_h,
    fproj_h,
    lift_h,
    tlift_h,
    nbr_h,
    bnd_h,
    send_h,
    out_o,
    ind_o,
    est_o,
    init_v,
    rhs_v,
    coef_v,
    stiff_v,
    binv_v,
    fproj_v,
    lift_v,
    tlift_v,
    nbr_v,
    bnd_v,
    send_v,
    place,
    x3,
    work,
    lat,
    jumps,
    jsplit,
    resid,
    direc,
    image,
    w_vol,
    w_lift,
    w_inv,
    rim_out,
    rim_in,
    end_in,
    row_a,
    row_b,
    load_sem,
    end_send,
    end_recv,
    rim_send,
    rim_recv,
    sum_send,
    sum_recv,
):
    t = lax.axis_index("tm")
    p = lax.axis_index("space")

    barrier = pltpu.get_barrier_semaphore()
    for d in range(1, nt):
        pl.semaphore_signal(barrier, inc=1, device_id={"tm": lax.rem(t + d, nt)}, device_id_type=MESH)
    for d in range(1, ns):
        pl.semaphore_signal(barrier, inc=1, device_id={"space": lax.rem(p + d, ns)}, device_id_type=MESH)

    loads = {}
    for n, (name, src, dst) in enumerate(
        (
            ("nbr", nbr_h, nbr_v),
            ("send", send_h, send_v),
            ("bnd", bnd_h, bnd_v),
            ("init", init_h.at[0], init_v),
            ("coef", coef_h, coef_v),
            ("fproj", fproj_h, fproj_v),
            ("stiff", stiff_h, stiff_v),
            ("lift", lift_h, lift_v),
            ("tlift", tlift_h, tlift_v),
            ("rhs", rhs_h.at[0], rhs_v),
            ("binv", binv_h, binv_v),
        )
    ):
        loads[name] = pltpu.make_async_copy(src, dst, load_sem.at[n])
        loads[name].start()

    loads["nbr"].wait()
    loads["send"].wait()
    loads["bnd"].wait()

    def table(ref, f):
        return jnp.concatenate([ref[f : f + 1, layer(k)] for k in range(8)], axis=0)

    first = p == 0
    lower = send_v[0:1, :] & (E - 1)
    upper = send_v[1:2, :] & (E - 1)
    chain_table = jnp.where(first, table(nbr_v, 0), table(nbr_v, 1)) & (E - 1)
    chain = [jnp.where(first, upper, lower)]
    for k in range(1, LAYERS):
        chain.append(lookup(chain_table, chain[-1]))
    slots = [jnp.where(first, chain[LAYERS - 1 - k], chain[k]) for k in range(LAYERS)]

    pl.semaphore_wait(barrier, nt + ns - 2)
    up = {"tm": lax.rem(t + 1, nt)}
    upper_part = {"space": lax.rem(p + 1, ns)}
    lower_part = {"space": lax.rem(p + ns - 1, ns)}

    def send_end(k, src):
        copy = pltpu.make_async_remote_copy(
            src_ref=src,
            dst_ref=end_in.at[k],
            send_sem=end_send.at[k],
            recv_sem=end_recv.at[k],
            device_id=up,
            device_id_type=MESH,
        )
        copy.start()
        return copy

    def send_rims(k):
        copies = []
        for side, device in ((0, upper_part), (1, lower_part)):
            copy = pltpu.make_async_remote_copy(
                src_ref=rim_out.at[k, side],
                dst_ref=rim_in.at[k, side],
                send_sem=rim_send.at[k, side],
                recv_sem=rim_recv.at[k, side],
                device_id=device,
                device_id_type=MESH,
            )
            copy.start()
            copies.append(copy)
        return copies

    loads["init"].wait()
    end_copy = send_end(0, init_v.at[pl.ds(H, H)])

    for k in range(LAYERS):
        place[:, layer(k)] = one_hot(iota((E, NB), 0) == slots[k])
    base_col = column(slots[0])
    top_col = column(slots[LAYERS - 1])
    out_map = one_hot(top_col == upper)
    in_map = one_hot(column(upper) == slots[LAYERS - 1])
    lateral = []
    for f in range(2, 6):
        target = lookup(table(nbr_v, f) & (E - 1), slots[0])
        wall = lookup(table(bnd_v, f), slots[0])
        lateral.append(one_hot((base_col == target) & (wall == 0)))
    blank = jnp.zeros((NB, NB), BF16)
    lat_maps = [
        jnp.concatenate(
            [
                jnp.concatenate([lateral[2 * g], blank], axis=1),
                jnp.concatenate([blank, lateral[2 * g + 1]], axis=1),
            ],
            axis=0,
        )
        for g in range(2)
    ]

    loads["fproj"].wait()
    loads["stiff"].wait()
    loads["lift"].wait()
    loads["tlift"].wait()
    loads["binv"].wait()
    row, col = iota((R, R), 0), iota((R, R), 1)
    to_face = one_hot(col == (row & 31) * 6 + (row >> 5))
    from_face = one_hot(row == (col & 31) * 6 + (col >> 5))
    both = dot(to_face, jnp.concatenate(split(fproj_v[...]), axis=1)).astype(BF16)
    fh, fl = both[:, :D], both[:, D:]
    sh, sl = split(stiff_v[...])
    w_vol[0:R, :] = jnp.concatenate([fh, fh, fl], axis=1)
    w_vol[R : R + D, :] = jnp.concatenate([sh, sh, sl], axis=1)
    both = dot(jnp.concatenate(split(lift_v[...]), axis=0), from_face).astype(BF16)
    th, tl = split(tlift_v[...])
    lh = jnp.concatenate([both[:D], th], axis=1)
    ll = jnp.concatenate([both[D:], tl], axis=1)
    w_lift[...] = jnp.concatenate([lh, lh, ll], axis=1)
    bh, bl = split(binv_v[...])
    w_inv[...] = jnp.concatenate([bh, bh, bl], axis=1)

    ih, il = split(init_v[...])
    loads["coef"].wait()
    coef = coef_v[...]
    ch = coef.astype(BF16)
    rest = coef - ch.astype(F32)
    cm = rest.astype(BF16)
    cl = (rest - cm.astype(F32)).astype(BF16)
    moved = dot(jnp.concatenate([ih, il, ch, cm, cl, jnp.zeros((13, E), BF16)], axis=0), place[...])
    coef = moved[2 * D : 2 * D + 1] + moved[2 * D + 1 : 2 * D + 2] + moved[2 * D + 2 : 2 * D + 3]
    xh = moved[0:D].astype(BF16)
    x3[0:D, :] = xh
    x3[D : 2 * D, :] = moved[D : 2 * D].astype(BF16)
    x3[2 * D : 3 * D, :] = xh
    start = moved[0:H] + moved[D : D + H]

    def traces_of(k):
        work[...] = dot(w_vol[...], x3[...])
        rim_out[k, 1] = work[0:FD, layer(0)]
        th, tl = split(work[FD : 2 * FD, layer(LAYERS - 1)])
        turned = dot(jnp.concatenate([th, tl], axis=0), out_map)
        rim_out[k, 0] = turned[:FD] + turned[FD:]

    def lateral_jumps(k):
        for g in range(2):
            a, b = 2 + 2 * g, 3 + 2 * g
            for x in range(LAYERS):
                for side, f in ((0, b), (1, a)):
                    th, tl = split(work[f * FD : (f + 1) * FD, layer(x)])
                    lat[x * 2 * FD : x * 2 * FD + FD, layer(side)] = th
                    lat[x * 2 * FD + FD : (x + 1) * 2 * FD, layer(side)] = tl
            seen = dot(lat[...], lat_maps[g])
            for x in range(LAYERS):
                both = seen[x * 2 * FD : x * 2 * FD + FD] + seen[x * 2 * FD + FD : (x + 1) * 2 * FD]
                for side, f in ((0, a), (1, b)):
                    jumps[k, f * FD : (f + 1) * FD, layer(x)] = work[f * FD : (f + 1) * FD, layer(x)] - both[:, layer(side)]
        for x in range(1, LAYERS):
            jumps[k, 0:FD, layer(x)] = work[0:FD, layer(x)] - work[FD : 2 * FD, layer(x - 1)]
            jumps[k, FD : 2 * FD, layer(x - 1)] = work[FD : 2 * FD, layer(x - 1)] - work[0:FD, layer(x)]

    def rim_jumps(k, copies):
        copies[0].wait_recv()
        copies[1].wait_recv()
        from_lower = jnp.where(p == 0, 0.0, rim_in[k, 0])
        jumps[k, 0:FD, layer(0)] = work[0:FD, layer(0)] - from_lower
        th, tl = split(rim_in[k, 1])
        turned = dot(jnp.concatenate([th, tl], axis=0), in_map)
        from_upper = jnp.where(p == ns - 1, 0.0, turned[:FD] + turned[FD:])
        last = layer(LAYERS - 1)
        jumps[k, FD : 2 * FD, last] = work[FD : 2 * FD, last] - from_upper

    def apply(k):
        jh, jl = split(jumps[k])
        jsplit[0:256, :] = jh
        jsplit[256:512, :] = jl
        jsplit[512:768, :] = jh
        return coef * work[R : R + D, :] + dot(w_lift[...], jsplit[...])

    traces_of(0)
    rims = send_rims(0)
    loads["rhs"].wait()
    moved = dot(jnp.concatenate(split(rhs_v[...]), axis=0), place[...])
    resid[...] = moved[:D] + moved[D:]
    lateral_jumps(0)
    rim_jumps(0, rims)
    end_copy.wait_recv()
    moved = dot(jnp.concatenate(split(end_in[0]), axis=0), place[...])
    jumps[0, R:, :] = start - jnp.where(t == 0, 0.0, moved[:H] + moved[H:])
    residual = resid[...] - apply(0)
    resid[...] = residual
    rh, rl = split(residual)
    x3[0:D, :] = rh
    x3[D : 2 * D, :] = rl
    x3[2 * D : 3 * D, :] = rh
    direction = dot(w_inv[...], x3[...]) / coef
    direc[...] = direction
    end_copy2 = send_end(1, direc.at[pl.ds(H, H)])
    dh, dl = split(direction)
    x3[0:D, :] = dh
    x3[D : 2 * D, :] = dl
    x3[2 * D : 3 * D, :] = dh

    traces_of(1)
    rims2 = send_rims(1)
    lateral_jumps(1)
    rim_jumps(1, rims2)
    end_copy2.wait_recv()
    jumps[1, R:, :] = direc[0:H, :] - jnp.where(t == 0, 0.0, end_in[1])
    image[...] = apply(1)

    def over(x):
        return jnp.sum(x, axis=0, keepdims=True)

    im, r = image[...], resid[...]
    cross = over(r * im)
    square = over(im * im)
    base = over(r * r) + 0.5 * over(jumps[0, :R] * jumps[0, :R]) + over(jumps[0, R:] * jumps[0, R:])
    mixed = over(jumps[0, :R] * jumps[1, :R]) + 2.0 * over(jumps[0, R:] * jumps[1, R:]) - 2.0 * cross
    quad = square + 0.5 * over(jumps[1, :R] * jumps[1, :R]) + over(jumps[1, R:] * jumps[1, R:])
    rows = jnp.concatenate([cross, square, base, mixed, quad, jnp.zeros((3, E), F32)], axis=0)
    folded = rows[:, layer(0)]
    for k in range(1, 8):
        folded = folded + rows[:, layer(k)]
    sums = jnp.sum(folded, axis=1, keepdims=True)
    diagonal = iota((8, NB), 0) == iota((8, NB), 1)
    message = jnp.sum(jnp.where(diagonal, sums, 0.0), axis=0, keepdims=True)

    def exchange(buf, me, count, axis, n):
        copies = []
        for d in range(1, count):
            copy = pltpu.make_async_remote_copy(
                src_ref=buf.at[me],
                dst_ref=buf.at[me],
                send_sem=sum_send.at[n],
                recv_sem=sum_recv.at[n],
                device_id={axis: lax.rem(me + d, count)},
                device_id_type=MESH,
            )
            copy.start()
        return pltpu.make_async_copy(buf.at[pl.ds(0, count - 1)], buf.at[pl.ds(0, count - 1)], sum_recv.at[n])

    row_a[t] = message
    got = exchange(row_a, t, nt, "tm", 0)
    a0, rest = split_rows(rows)
    back = lax.dot_general(
        jnp.concatenate([dh, dl, a0, rest], axis=0),
        place[...],
        (((1,), (1,)), ((), ())),
        preferred_element_type=F32,
    )
    got.wait()
    total = row_a[0]
    for d in range(1, nt):
        total = total + row_a[d]
    row_b[p] = total
    got_b = exchange(row_b, p, ns, "space", 1)
    got_b.wait()
    total = row_b[0]
    for d in range(1, ns):
        total = total + row_b[d]
    cross, square, base, mixed, quad = (total[0:1, k : k + 1] for k in range(5))
    step = cross / square
    eta_total = base + step * mixed + step * step * quad
    out_o[0] = init_v[...] + step * (back[:D] + back[D : 2 * D])
    parts = back[2 * D : 2 * D + 8] + back[2 * D + 8 : 2 * D + 16] + back[2 * D + 16 : 2 * D + 24]
    eta = parts[2:3] + step * parts[3:4] + step * step * parts[4:5]
    count = float(E * nt * ns)
    ind_o[...] = eta * count / eta_total
    est_o[...] = jnp.broadcast_to(jnp.sqrt(eta_total / count), (1, NB))

    end_copy.wait_send()
    end_copy2.wait_send()
    for copy in rims + rims2:
        copy.wait_send()
    for buf, count, n in ((row_a, nt, 0), (row_b, ns, 1)):
        sent = buf.at[pl.ds(0, count - 1)]
        pltpu.make_async_copy(sent, sent, sum_send.at[n]).wait()


def split_rows(rows):
    high, rest = rows.astype(BF16), None
    rest = rows - high.astype(F32)
    mid = rest.astype(BF16)
    low = (rest - mid.astype(F32)).astype(BF16)
    return high, jnp.concatenate([mid, low], axis=0)


def on_device(nt, ns, initial, rhs, coef, stiffness, block_inverse, face_proj, lift, time_lift, neighbour, boundary, send_list):
    vmem = pltpu.VMEM
    any_spec = pl.BlockSpec(memory_space=pl.ANY)
    vmem_spec = pl.BlockSpec(memory_space=vmem)
    smoothed, indicator, estimate = pl.pallas_call(
        functools.partial(kernel, nt, ns),
        out_shape=(
            jax.ShapeDtypeStruct((1, D, E), F32),
            jax.ShapeDtypeStruct((1, E), F32),
            jax.ShapeDtypeStruct((1, NB), F32),
        ),
        in_specs=[any_spec] * 11,
        out_specs=[vmem_spec] * 3,
        scratch_shapes=[
            vmem((D, E), F32),
            vmem((D, E), F32),
            vmem((1, E), F32),
            vmem((D, D), F32),
            vmem((D, D), F32),
            vmem((R, D), F32),
            vmem((D, R), F32),
            vmem((D, H), F32),
            vmem((6, E), jnp.int32),
            vmem((6, E), jnp.int32),
            vmem((2, NB), jnp.int32),
            vmem((E, E), BF16),
            vmem((3 * D, E), BF16),
            vmem((R + D, E), F32),
            vmem((LAYERS * 2 * FD, 2 * NB), BF16),
            vmem((2, 256, E), F32),
            vmem((768, E), BF16),
            vmem((D, E), F32),
            vmem((D, E), F32),
            vmem((D, E), F32),
            vmem((R + D, 3 * D), BF16),
            vmem((D, 768), BF16),
            vmem((D, 3 * D), BF16),
            vmem((2, 2, FD, NB), F32),
            vmem((2, 2, FD, NB), F32),
            vmem((2, H, E), F32),
            vmem((nt, 1, NB), F32),
            vmem((ns, 1, NB), F32),
            pltpu.SemaphoreType.DMA((11,)),
            pltpu.SemaphoreType.DMA((2,)),
            pltpu.SemaphoreType.DMA((2,)),
            pltpu.SemaphoreType.DMA((2, 2)),
            pltpu.SemaphoreType.DMA((2, 2)),
            pltpu.SemaphoreType.DMA((2,)),
            pltpu.SemaphoreType.DMA((2,)),
        ],
        compiler_params=pltpu.CompilerParams(collective_id=0, has_side_effects=True, vmem_limit_bytes=48 * 1024 * 1024),
        cost_estimate=pl.CostEstimate(flops=4 * 10**9, bytes_accessed=3 * 2**20, transcendentals=0),
    )(
        initial,
        rhs,
        coef.reshape(1, E),
        stiffness,
        block_inverse,
        face_proj,
        lift,
        time_lift,
        neighbour,
        boundary,
        send_list.reshape(2, NB),
    )
    return smoothed, indicator, estimate[0, :1]


def solution(mesh):
    return jax.shard_map(
        functools.partial(on_device, mesh.shape["tm"], mesh.shape["space"]),
        mesh=mesh,
        in_specs=(
            P("tm", None, "space"),
            P("tm", None, "space"),
            P("space"),
            P(),
            P(),
            P(),
            P(),
            P(),
            P(None, "space"),
            P(None, "space"),
            P("space"),
        ),
        out_specs=(P("tm", None, "space"), P("tm", "space"), P()),
        check_vma=False,
    )
```

```python
import functools

import jax
import jax.numpy as jnp
from jax import lax
from jax.experimental import pallas as pl
from jax.experimental.pallas import tpu as pltpu
from jax.sharding import PartitionSpec as P

MESH = pl.DeviceIdType.MESH
F32 = jnp.float32
BF16 = jnp.bfloat16
D = 128
H = 64
FD = 32
R = 192
LAYERS = 8
NB = 128
E = 1024


def split(x):
    high = x.astype(BF16)
    return high, (x - high.astype(F32)).astype(BF16)


def dot(a, b):
    return jnp.dot(a, b, preferred_element_type=F32)


def iota(shape, dim):
    return lax.broadcasted_iota(jnp.int32, shape, dim)


def one_hot(mask):
    return jnp.where(mask, 1.0, 0.0).astype(BF16)


def column(row):
    eye = iota((NB, NB), 0) == iota((NB, NB), 1)
    return jnp.sum(jnp.where(eye, jnp.broadcast_to(row, (NB, NB)), 0), axis=1, keepdims=True)


def lookup(table, index):
    lane = jnp.broadcast_to(index & 127, (8, NB))
    line = jnp.broadcast_to(index >> 7, (8, NB))
    found = jnp.take_along_axis(table, lane, axis=1)
    return jnp.sum(jnp.where(line == iota((8, NB), 0), found, 0), axis=0, keepdims=True)


def layer(k):
    return slice(k * NB, (k + 1) * NB)


def rounds(n):
    out, known = [], 1
    while known < n // 2:
        out.append(known)
        known *= 2
    return out


def near(n):
    return (1,) if n == 2 else (1, n - 1)


def stack3(x):
    high, low = split(x)
    return jnp.concatenate([high, low, high], axis=0)


def over(x):
    return jnp.sum(x, axis=0, keepdims=True)


PARTS = (0, 3, 1, 2)
W = 256
CUT = 768


def part(q):
    return slice(q * W, (q + 1) * W)


def kernel(
    nt,
    ns,
    init_h,
    rhs_h,
    coef_h,
    stiff_h,
    binv_h,
    fproj_h,
    lift_h,
    tlift_h,
    nbr_h,
    bnd_h,
    send_h,
    dir_o,
    eta_o,
    tot_o,
    init_v,
    rhs_v,
    coef_v,
    stiff_v,
    binv_v,
    fproj_v,
    lift_v,
    tlift_v,
    nbr_v,
    bnd_v,
    send_v,
    place,
    xs,
    x3,
    r3,
    t3,
    work,
    lat,
    jumps,
    jsplit,
    pre,
    bpre,
    moved_end,
    resid,
    direc,
    rows,
    w_vol,
    w_lift,
    w_time,
    w_inv,
    w_both,
    rim_out,
    rim_in,
    end_in,
    row_a,
    row_b,
    load_sem,
    end_send,
    end_recv,
    rim_send,
    rim_recv,
    sum_send,
    sum_recv,
    known_sem,
):
    t = lax.axis_index("tm")
    p = lax.axis_index("space")
    axes = (("tm", t, nt, 0), ("space", p, ns, len(rounds(nt))))

    barrier = pltpu.get_barrier_semaphore()
    for axis, me, n, _ in axes:
        for d in near(n):
            pl.semaphore_signal(barrier, inc=1, device_id={axis: lax.rem(me + d, n)}, device_id_type=MESH)

    def know(k):
        for axis, me, n, base in axes:
            reach = rounds(n)
            if 0 < k <= len(reach):
                pl.semaphore_wait(known_sem.at[base + k - 1], 2)
            if k < len(reach):
                for d in (reach[k], n - reach[k]):
                    pl.semaphore_signal(known_sem.at[base + k], inc=1, device_id={axis: lax.rem(me + d, n)}, device_id_type=MESH)

    loads = {}
    for n, (name, src, dst) in enumerate(
        (
            ("send", send_h, send_v),
            ("init", init_h.at[0], init_v),
            ("fproj", fproj_h, fproj_v),
            ("nbr", nbr_h, nbr_v),
            ("bnd", bnd_h, bnd_v),
            ("coef", coef_h, coef_v),
            ("stiff", stiff_h, stiff_v),
            ("lift", lift_h, lift_v),
            ("tlift", tlift_h, tlift_v),
            ("binv", binv_h, binv_v),
            ("rhs", rhs_h.at[0], rhs_v),
        )
    ):
        loads[name] = pltpu.make_async_copy(src, dst, load_sem.at[n])
        loads[name].start()

    row, col = iota((R, R), 0), iota((R, R), 1)
    to_face = one_hot(col == (row & 31) * 6 + (row >> 5))
    loads["send"].wait()
    lower = send_v[0:1, :] & (E - 1)
    upper = send_v[1:2, :] & (E - 1)
    column_ids = iota((E, NB), 0)
    ends = jnp.concatenate([one_hot(column_ids == lower), one_hot(column_ids == upper)], axis=1)
    loads["fproj"].wait()
    both = dot(to_face, jnp.concatenate(split(fproj_v[...]), axis=1)).astype(BF16)
    fh, fl = both[:, :D], both[:, D:]
    w_vol[0:R, :] = jnp.concatenate([fh, fh, fl], axis=1)

    loads["init"].wait()
    ih, il = split(init_v[...])
    xs[0:D, :] = ih
    xs[D : 2 * D, :] = il
    picked = dot(xs[0 : 2 * D, :], ends).astype(BF16)
    rim = dot(w_vol[0 : 2 * FD, :], jnp.concatenate([picked[:D], picked[D:], picked[:D]], axis=0))
    rim_out[0, 1] = rim[0:FD, 0:NB]
    rim_out[0, 0] = rim[FD : 2 * FD, NB : 2 * NB]

    loads["nbr"].wait()
    loads["bnd"].wait()

    def table(ref, f):
        return jnp.concatenate([ref[f : f + 1, layer(k)] for k in range(8)], axis=0)

    first = p == 0
    chain_table = jnp.where(first, table(nbr_v, 0), table(nbr_v, 1)) & (E - 1)
    chain = [jnp.where(first, upper, lower)]
    for k in range(1, LAYERS):
        chain.append(lookup(chain_table, chain[-1]))
    slots = [jnp.where(first, chain[LAYERS - 1 - k], chain[k]) for k in range(LAYERS)]

    pl.semaphore_wait(barrier, len(near(nt)) + len(near(ns)))
    up = {"tm": lax.rem(t + 1, nt)}
    upper_part = {"space": lax.rem(p + 1, ns)}
    lower_part = {"space": lax.rem(p + ns - 1, ns)}

    def send_end(k, n, src, columns):
        copy = pltpu.make_async_remote_copy(
            src_ref=src.at[pl.ds(H, H), columns],
            dst_ref=end_in.at[k, :, columns],
            send_sem=end_send.at[k, n],
            recv_sem=end_recv.at[k, n],
            device_id=up,
            device_id_type=MESH,
        )
        copy.start()
        return copy

    def send_rims(k):
        copies = []
        for side, device in ((0, upper_part), (1, lower_part)):
            copy = pltpu.make_async_remote_copy(
                src_ref=rim_out.at[k, side],
                dst_ref=rim_in.at[k, side],
                send_sem=rim_send.at[k, side],
                recv_sem=rim_recv.at[k, side],
                device_id=device,
                device_id_type=MESH,
            )
            copy.start()
            copies.append(copy)
        return copies

    rims = send_rims(0)
    end_copies = [send_end(0, 0, init_v, pl.ds(0, CUT)), send_end(0, 1, init_v, pl.ds(CUT, E - CUT))]
    know(0)

    for k in range(LAYERS):
        place[:, layer(k)] = one_hot(column_ids == slots[k])
    base_col = column(slots[0])
    top_col = column(slots[LAYERS - 1])
    out_map = one_hot(top_col == upper)
    in_map = one_hot(column(upper) == slots[LAYERS - 1])
    lateral = []
    for f in range(2, 6):
        target = lookup(table(nbr_v, f) & (E - 1), slots[0])
        wall = lookup(table(bnd_v, f), slots[0])
        lateral.append(one_hot((base_col == target) & (wall == 0)))
    blank = jnp.zeros((NB, NB), BF16)
    lat_maps = [
        jnp.concatenate(
            [
                jnp.concatenate([lateral[2 * g], blank], axis=1),
                jnp.concatenate([blank, lateral[2 * g + 1]], axis=1),
            ],
            axis=0,
        )
        for g in range(2)
    ]

    loads["stiff"].wait()
    sh, sl = split(stiff_v[...])
    w_vol[R : R + D, :] = jnp.concatenate([sh, sh, sl], axis=1)

    loads["coef"].wait()
    coef = coef_v[...]
    ch = coef.astype(BF16)
    rest = coef - ch.astype(F32)
    cm = rest.astype(BF16)
    cl = (rest - cm.astype(F32)).astype(BF16)
    xs[2 * D : 2 * D + 16, :] = jnp.concatenate([ch, cm, cl, jnp.zeros((13, E), BF16)], axis=0)
    moved = dot(xs[...], place[...])
    coef = moved[2 * D : 2 * D + 1] + moved[2 * D + 1 : 2 * D + 2] + moved[2 * D + 2 : 2 * D + 3]
    inverse_coef = 1.0 / coef
    xh = moved[0:D].astype(BF16)
    x3[0:D, :] = xh
    x3[D : 2 * D, :] = moved[D : 2 * D].astype(BF16)
    x3[2 * D : 3 * D, :] = xh
    start = moved[0:H] + moved[D : D + H]

    know(1)

    def wide(high, low):
        return jnp.concatenate([high, high, low], axis=0).astype(F32).T.astype(BF16)

    loads["lift"].wait()
    both = dot(to_face, jnp.concatenate(split(lift_v[...]), axis=1))
    w_lift[...] = wide(both[:, :D], both[:, D:])
    loads["tlift"].wait()
    th, tl = split(tlift_v[...])
    w_time[...] = wide(th, tl)
    loads["binv"].wait()
    bh, bl = split(binv_v[...])
    w_inv[...] = jnp.concatenate([bh, bh, bl], axis=1)
    both = lax.dot_general(
        jnp.concatenate([th, tl, th], axis=1), w_inv[...], (((1,), (1,)), ((), ())), preferred_element_type=F32
    )
    w_both[...] = wide(*split(both))

    def lateral_jumps(k):
        for g in range(2):
            a, b = 2 + 2 * g, 3 + 2 * g
            for x in range(LAYERS):
                for side, f in ((0, b), (1, a)):
                    high, low = split(work[f * FD : (f + 1) * FD, layer(x)])
                    lat[x * 2 * FD : x * 2 * FD + FD, layer(side)] = high
                    lat[x * 2 * FD + FD : (x + 1) * 2 * FD, layer(side)] = low
            seen = dot(lat[...], lat_maps[g])
            for x in range(LAYERS):
                both = seen[x * 2 * FD : x * 2 * FD + FD] + seen[x * 2 * FD + FD : (x + 1) * 2 * FD]
                for side, f in ((0, a), (1, b)):
                    jumps[k, f * FD : (f + 1) * FD, layer(x)] = work[f * FD : (f + 1) * FD, layer(x)] - both[:, layer(side)]
        for x in range(1, LAYERS):
            jumps[k, 0:FD, layer(x)] = work[0:FD, layer(x)] - work[FD : 2 * FD, layer(x - 1)]
            jumps[k, FD : 2 * FD, layer(x - 1)] = work[FD : 2 * FD, layer(x - 1)] - work[0:FD, layer(x)]

    def rim_jumps(k, copies):
        copies[0].wait_recv()
        copies[1].wait_recv()
        from_lower = jnp.where(p == 0, 0.0, rim_in[k, 0])
        jumps[k, 0:FD, layer(0)] = work[0:FD, layer(0)] - from_lower
        turned = dot(jnp.concatenate(split(rim_in[k, 1]), axis=0), in_map)
        from_upper = jnp.where(p == ns - 1, 0.0, turned[:FD] + turned[FD:])
        last = layer(LAYERS - 1)
        jumps[k, FD : 2 * FD, last] = work[FD : 2 * FD, last] - from_upper

    def apply_local(k):
        jsplit[...] = stack3(jumps[k, 0:R])
        return coef * work[R : R + D, :] + dot(w_lift[...], jsplit[...])

    work[...] = dot(w_vol[...], x3[...])
    lateral_jumps(0)
    know(2)
    loads["rhs"].wait()
    moved = dot(jnp.concatenate(split(rhs_v[...]), axis=0), place[...])
    pre[...] = moved[:D] + moved[D:]
    rim_jumps(0, rims)
    pre[...] = pre[...] - apply_local(0)
    r3[...] = stack3(pre[...])
    bpre[...] = dot(w_inv[...], r3[...]) * inverse_coef
    know(3)

    end_copies[0].wait_recv()
    moved_end[...] = dot(jnp.concatenate(split(end_in[0, :, 0:CUT]), axis=0), place[0:CUT, :])
    end_copies[1].wait_recv()
    late = jnp.concatenate(split(end_in[0, :, CUT:E]), axis=0)
    dir_copies = {}
    for q in PARTS:
        c = part(q)
        moved = moved_end[:, c] + dot(late, place[CUT:E, c])
        jump = start[:, c] - jnp.where(t == 0, 0.0, moved[:H] + moved[H:])
        jumps[0, R:, c] = jump
        t3[:, c] = stack3(jump)
        direction = bpre[:, c] - dot(w_both[...], t3[:, c]) * inverse_coef[:, c]
        direc[:, c] = direction
        dir_copies[q] = send_end(1, q, direc, pl.ds(q * W, W))
        x3[:, c] = stack3(direction)

    for q in PARTS:
        work[:, part(q)] = dot(w_vol[...], x3[:, part(q)])
        if q == 3:
            rim_out[1, 1] = work[0:FD, layer(0)]
            turned = dot(jnp.concatenate(split(work[FD : 2 * FD, layer(LAYERS - 1)]), axis=0), out_map)
            rim_out[1, 0] = turned[:FD] + turned[FD:]
            rims2 = send_rims(1)
    know(4)
    residual = pre[...] - dot(w_time[...], t3[...])
    resid[...] = residual
    rows[2:3, :] = over(residual * residual) + 0.5 * over(jumps[0, :R] * jumps[0, :R]) + over(jumps[0, R:] * jumps[0, R:])
    lateral_jumps(1)
    rim_jumps(1, rims2)
    pre[...] = apply_local(1)
    mixed = over(jumps[0, :R] * jumps[1, :R])
    quad = 0.5 * over(jumps[1, :R] * jumps[1, :R])
    folded = jnp.zeros((8, NB), F32)
    for q in PARTS:
        c = part(q)
        dir_copies[q].wait_recv()
        jump = direc[0:H, c] - jnp.where(t == 0, 0.0, end_in[1, :, c])
        image = pre[:, c] + dot(w_time[...], stack3(jump))
        cross = over(resid[:, c] * image)
        square = over(image * image)
        part_rows = jnp.concatenate(
            [
                cross,
                square,
                rows[2:3, c],
                mixed[:, c] + 2.0 * over(jumps[0, R:, c] * jump) - 2.0 * cross,
                quad[:, c] + square + over(jump * jump),
                jnp.zeros((3, W), F32),
            ],
            axis=0,
        )
        rows[:, c] = part_rows
        folded = folded + part_rows[:, :NB] + part_rows[:, NB:]
    sums = jnp.sum(folded, axis=1, keepdims=True)
    diagonal = iota((8, NB), 0) == iota((8, NB), 1)
    message = jnp.sum(jnp.where(diagonal, sums, 0.0), axis=0, keepdims=True)

    def exchange(buf, me, count, axis, n):
        for d in range(1, count):
            pltpu.make_async_remote_copy(
                src_ref=buf.at[me],
                dst_ref=buf.at[me],
                send_sem=sum_send.at[n],
                recv_sem=sum_recv.at[n],
                device_id={axis: lax.rem(me + d, count)},
                device_id_type=MESH,
            ).start()
        others = buf.at[pl.ds(0, count - 1)]
        return pltpu.make_async_copy(others, others, sum_recv.at[n])

    row_a[t] = message
    got = exchange(row_a, t, nt, "tm", 0)
    eh = rows[...].astype(BF16)
    rest = rows[...] - eh.astype(F32)
    em = rest.astype(BF16)
    el = (rest - em.astype(F32)).astype(BF16)
    back = lax.dot_general(
        jnp.concatenate([x3[0 : 2 * D, :], eh, em, el, jnp.zeros((8, E), BF16)], axis=0),
        place[...],
        (((1,), (1,)), ((), ())),
        preferred_element_type=F32,
    )
    dir_o[...] = back[:D] + back[D : 2 * D]
    eta_o[...] = back[2 * D : 2 * D + 8] + back[2 * D + 8 : 2 * D + 16] + back[2 * D + 16 : 2 * D + 24]
    got.wait()
    total = row_a[0]
    for d in range(1, nt):
        total = total + row_a[d]
    row_b[p] = total
    exchange(row_b, p, ns, "space", 1).wait()
    total = row_b[0]
    for d in range(1, ns):
        total = total + row_b[d]
    tot_o[...] = total

    for copy in end_copies + [dir_copies[q] for q in PARTS] + rims + rims2:
        copy.wait_send()
    for buf, count, n in ((row_a, nt, 0), (row_b, ns, 1)):
        sent = buf.at[pl.ds(0, count - 1)]
        pltpu.make_async_copy(sent, sent, sum_send.at[n]).wait()


def finish(count, init_v, dir_v, eta_v, tot_v, out_o, ind_o, est_o):
    cross, square, base, mixed, quad = (tot_v[0:1, k : k + 1] for k in range(5))
    step = cross / square
    eta_total = base + step * mixed + step * step * quad
    out_o[0] = init_v[0] + step * dir_v[...]
    eta = eta_v[2:3] + step * eta_v[3:4] + step * step * eta_v[4:5]
    ind_o[...] = eta * count / eta_total
    est_o[...] = jnp.broadcast_to(jnp.sqrt(eta_total / count), (1, NB))


def on_device(nt, ns, initial, rhs, coef, stiffness, block_inverse, face_proj, lift, time_lift, neighbour, boundary, send_list):
    vmem = pltpu.VMEM
    hbm_spec = pl.BlockSpec(memory_space=pltpu.HBM)
    vmem_spec = pl.BlockSpec(memory_space=vmem)
    dma = pltpu.SemaphoreType.DMA
    direction, eta, totals = pl.pallas_call(
        functools.partial(kernel, nt, ns),
        out_shape=(
            jax.ShapeDtypeStruct((D, E), F32),
            jax.ShapeDtypeStruct((8, E), F32),
            jax.ShapeDtypeStruct((1, NB), F32),
        ),
        in_specs=[hbm_spec] * 11,
        out_specs=[vmem_spec] * 3,
        scratch_shapes=[
            vmem((D, E), F32),
            vmem((D, E), F32),
            vmem((1, E), F32),
            vmem((D, D), F32),
            vmem((D, D), F32),
            vmem((R, D), F32),
            vmem((R, D), F32),
            vmem((H, D), F32),
            vmem((6, E), jnp.int32),
            vmem((6, E), jnp.int32),
            vmem((2, NB), jnp.int32),
            vmem((E, E), BF16),
            vmem((2 * D + 16, E), BF16),
            vmem((3 * D, E), BF16),
            vmem((3 * D, E), BF16),
            vmem((3 * H, E), BF16),
            vmem((R + D, E), F32),
            vmem((LAYERS * 2 * FD, 2 * NB), BF16),
            vmem((2, 256, E), F32),
            vmem((3 * R, E), BF16),
            vmem((D, E), F32),
            vmem((D, E), F32),
            vmem((2 * H, E), F32),
            vmem((D, E), F32),
            vmem((D, E), F32),
            vmem((8, E), F32),
            vmem((R + D, 3 * D), BF16),
            vmem((D, 3 * R), BF16),
            vmem((D, 3 * H), BF16),
            vmem((D, 3 * D), BF16),
            vmem((D, 3 * H), BF16),
            vmem((2, 2, FD, NB), F32),
            vmem((2, 2, FD, NB), F32),
            vmem((2, H, E), F32),
            vmem((nt, 1, NB), F32),
            vmem((ns, 1, NB), F32),
            dma((11,)),
            dma((2, 4)),
            dma((2, 4)),
            dma((2, 2)),
            dma((2, 2)),
            dma((2,)),
            dma((2,)),
            pltpu.SemaphoreType.REGULAR((max(1, len(rounds(nt)) + len(rounds(ns))),)),
        ],
        compiler_params=pltpu.CompilerParams(collective_id=0, has_side_effects=True, vmem_limit_bytes=40 * 1024 * 1024),
        cost_estimate=pl.CostEstimate(flops=4 * 10**9, bytes_accessed=3 * 2**20, transcendentals=0),
    )(
        *(
            pltpu.with_memory_space_constraint(x, pltpu.HBM)
            for x in (
                initial,
                rhs,
                coef.reshape(1, E),
                stiffness,
                block_inverse,
                face_proj,
                lift.T,
                time_lift.T,
                neighbour,
                boundary,
                send_list.reshape(2, NB),
            )
        )
    )
    smoothed, indicator, estimate = pl.pallas_call(
        functools.partial(finish, float(E * nt * ns)),
        out_shape=(
            jax.ShapeDtypeStruct((1, D, E), F32),
            jax.ShapeDtypeStruct((1, E), F32),
            jax.ShapeDtypeStruct((1, NB), F32),
        ),
        in_specs=[vmem_spec] * 4,
        out_specs=[vmem_spec] * 3,
        compiler_params=pltpu.CompilerParams(vmem_limit_bytes=8 * 1024 * 1024),
        cost_estimate=pl.CostEstimate(flops=3 * 10**5, bytes_accessed=2**20, transcendentals=0),
    )(initial, direction, eta, totals)
    return smoothed, indicator, estimate[0, :1]


def solution(mesh):
    return jax.shard_map(
        functools.partial(on_device, mesh.shape["tm"], mesh.shape["space"]),
        mesh=mesh,
        in_specs=(
            P("tm", None, "space"),
            P("tm", None, "space"),
            P("space"),
            P(),
            P(),
            P(),
            P(),
            P(),
            P(None, "space"),
            P(None, "space"),
            P("space"),
        ),
        out_specs=(P("tm", None, "space"), P("tm", "space"), P()),
        check_vma=False,
    )
```

```python
import functools

import jax
import jax.numpy as jnp
from jax import lax
from jax.experimental import pallas as pl
from jax.experimental.pallas import tpu as pltpu
from jax.sharding import PartitionSpec as P

MESH = pl.DeviceIdType.MESH
F32 = jnp.float32
BF16 = jnp.bfloat16
D = 128
H = 64
FD = 32
R = 192
LAYERS = 8
NB = 128
E = 1024


def split(x):
    high = x.astype(BF16)
    return high, (x - high.astype(F32)).astype(BF16)


def dot(a, b):
    return jnp.dot(a, b, preferred_element_type=F32)


def iota(shape, dim):
    return lax.broadcasted_iota(jnp.int32, shape, dim)


def one_hot(mask):
    return jnp.where(mask, 1.0, 0.0).astype(BF16)


def column(row):
    eye = iota((NB, NB), 0) == iota((NB, NB), 1)
    return jnp.sum(jnp.where(eye, jnp.broadcast_to(row, (NB, NB)), 0), axis=1, keepdims=True)


def lookup(table, index):
    lane = jnp.broadcast_to(index & 127, (8, NB))
    line = jnp.broadcast_to(index >> 7, (8, NB))
    found = jnp.take_along_axis(table, lane, axis=1)
    return jnp.sum(jnp.where(line == iota((8, NB), 0), found, 0), axis=0, keepdims=True)


def layer(k):
    return slice(k * NB, (k + 1) * NB)


def rounds(n):
    out, known = [], 1
    while known < n // 2:
        out.append(known)
        known *= 2
    return out


def near(n):
    return (1,) if n == 2 else (1, n - 1)


def stack3(x):
    high, low = split(x)
    return jnp.concatenate([high, low, high], axis=0)


def over(x):
    return jnp.sum(x, axis=0, keepdims=True)


PARTS = (0, 3, 1, 2)
W = 256
CUT = 768


def part(q):
    return slice(q * W, (q + 1) * W)


def kernel(
    nt,
    ns,
    init_h,
    rhs_h,
    coef_h,
    stiff_h,
    binv_h,
    fproj_h,
    lift_h,
    tlift_h,
    nbr_h,
    bnd_h,
    send_h,
    dir_o,
    eta_o,
    tot_o,
    init_v,
    rhs_v,
    coef_v,
    stiff_v,
    binv_v,
    fproj_v,
    lift_v,
    tlift_v,
    nbr_v,
    bnd_v,
    send_v,
    place,
    start_v,
    xs,
    x3,
    r3,
    t3,
    work,
    lat,
    jumps,
    jsplit,
    pre,
    bpre,
    moved_end,
    resid,
    direc,
    rows,
    w_vol,
    w_lift,
    w_time,
    w_inv,
    w_both,
    rim_out,
    rim_in,
    end_in,
    row_a,
    row_b,
    load_sem,
    end_send,
    end_recv,
    rim_send,
    rim_recv,
    sum_send,
    sum_recv,
    known_sem,
):
    t = lax.axis_index("tm")
    p = lax.axis_index("space")
    axes = (("tm", t, nt, 0), ("space", p, ns, len(rounds(nt))))

    barrier = pltpu.get_barrier_semaphore()
    for axis, me, n, _ in axes:
        for d in near(n):
            pl.semaphore_signal(barrier, inc=1, device_id={axis: lax.rem(me + d, n)}, device_id_type=MESH)

    def know(k, among=(0, 1)):
        for axis, me, n, base in (axes[i] for i in among):
            reach = rounds(n)
            if 0 < k <= len(reach):
                pl.semaphore_wait(known_sem.at[base + k - 1], 2)
            if k < len(reach):
                for d in (reach[k], n - reach[k]):
                    pl.semaphore_signal(known_sem.at[base + k], inc=1, device_id={axis: lax.rem(me + d, n)}, device_id_type=MESH)

    loads = {}
    for n, (name, src, dst) in enumerate(
        (
            ("send", send_h, send_v),
            ("init", init_h.at[0], init_v),
            ("fproj", fproj_h, fproj_v),
            ("nbr", nbr_h, nbr_v),
            ("bnd", bnd_h, bnd_v),
            ("coef", coef_h, coef_v),
            ("stiff", stiff_h, stiff_v),
            ("lift", lift_h, lift_v),
            ("tlift", tlift_h, tlift_v),
            ("binv", binv_h, binv_v),
            ("rhs", rhs_h.at[0], rhs_v),
        )
    ):
        loads[name] = pltpu.make_async_copy(src, dst, load_sem.at[n])
        loads[name].start()

    row, col = iota((R, R), 0), iota((R, R), 1)
    to_face = one_hot(col == (row & 31) * 6 + (row >> 5))
    loads["send"].wait()
    lower = send_v[0:1, :] & (E - 1)
    upper = send_v[1:2, :] & (E - 1)
    column_ids = iota((E, NB), 0)
    ends = jnp.concatenate([one_hot(column_ids == lower), one_hot(column_ids == upper)], axis=1)
    loads["fproj"].wait()
    both = dot(to_face, jnp.concatenate(split(fproj_v[...]), axis=1)).astype(BF16)
    fh, fl = both[:, :D], both[:, D:]
    w_vol[0:R, :] = jnp.concatenate([fh, fh, fl], axis=1)

    loads["init"].wait()
    ih, il = split(init_v[...])
    xs[0:D, :] = ih
    xs[D : 2 * D, :] = il
    picked = dot(xs[0 : 2 * D, :], ends).astype(BF16)
    rim = dot(w_vol[0 : 2 * FD, :], jnp.concatenate([picked[:D], picked[D:], picked[:D]], axis=0))
    rim_out[0, 1] = rim[0:FD, 0:NB]
    rim_out[0, 0] = rim[FD : 2 * FD, NB : 2 * NB]

    pl.semaphore_wait(barrier, len(near(nt)) + len(near(ns)))
    up = {"tm": lax.rem(t + 1, nt)}
    upper_part = {"space": lax.rem(p + 1, ns)}
    lower_part = {"space": lax.rem(p + ns - 1, ns)}

    def send_end(k, n, src, columns):
        copy = pltpu.make_async_remote_copy(
            src_ref=src.at[pl.ds(H, H), columns],
            dst_ref=end_in.at[k, :, columns],
            send_sem=end_send.at[k, n],
            recv_sem=end_recv.at[k, n],
            device_id=up,
            device_id_type=MESH,
        )
        copy.start()
        return copy

    def send_rims(k):
        copies = []
        for side, device in ((0, upper_part), (1, lower_part)):
            copy = pltpu.make_async_remote_copy(
                src_ref=rim_out.at[k, side],
                dst_ref=rim_in.at[k, side],
                send_sem=rim_send.at[k, side],
                recv_sem=rim_recv.at[k, side],
                device_id=device,
                device_id_type=MESH,
            )
            copy.start()
            copies.append(copy)
        return copies

    rims = send_rims(0)
    end_copies = [send_end(0, 0, init_v, pl.ds(0, CUT)), send_end(0, 1, init_v, pl.ds(CUT, E - CUT))]
    know(0)

    for name in ("nbr", "bnd", "coef", "stiff", "lift", "tlift", "binv"):
        loads[name].wait()

    def table(ref, f):
        return jnp.concatenate([ref[f : f + 1, layer(k)] for k in range(8)], axis=0)

    first = p == 0
    chain_table = jnp.where(first, table(nbr_v, 0), table(nbr_v, 1)) & (E - 1)
    chain = [jnp.where(first, upper, lower)]
    for k in range(1, LAYERS):
        chain.append(lookup(chain_table, chain[-1]))
    slots = [jnp.where(first, chain[LAYERS - 1 - k], chain[k]) for k in range(LAYERS)]

    base_col = column(slots[0])
    top_col = column(slots[LAYERS - 1])
    out_map = one_hot(top_col == upper)
    in_map = one_hot(column(upper) == slots[LAYERS - 1])
    lateral = []
    for f in range(2, 6):
        target = lookup(table(nbr_v, f) & (E - 1), slots[0])
        wall = lookup(table(bnd_v, f), slots[0])
        lateral.append(one_hot((base_col == target) & (wall == 0)))
    blank = jnp.zeros((NB, NB), BF16)
    lat_maps = [
        jnp.concatenate(
            [
                jnp.concatenate([lateral[2 * g], blank], axis=1),
                jnp.concatenate([blank, lateral[2 * g + 1]], axis=1),
            ],
            axis=0,
        )
        for g in range(2)
    ]

    sh, sl = split(stiff_v[...])
    w_vol[R : R + D, :] = jnp.concatenate([sh, sh, sl], axis=1)

    coef = coef_v[...]
    ch = coef.astype(BF16)
    rest = coef - ch.astype(F32)
    cm = rest.astype(BF16)
    cl = (rest - cm.astype(F32)).astype(BF16)
    xs[2 * D : 2 * D + 16, :] = jnp.concatenate([ch, cm, cl, jnp.zeros((13, E), BF16)], axis=0)
    for q in range(4):
        c = part(q)
        for k in (2 * q, 2 * q + 1):
            place[:, layer(k)] = one_hot(column_ids == slots[k])
        moved = dot(xs[...], place[:, c])
        coef_v[:, c] = moved[2 * D : 2 * D + 1] + moved[2 * D + 1 : 2 * D + 2] + moved[2 * D + 2 : 2 * D + 3]
        xh = moved[0:D].astype(BF16)
        x3[0:D, c] = xh
        x3[D : 2 * D, c] = moved[D : 2 * D].astype(BF16)
        x3[2 * D : 3 * D, c] = xh
        start_v[:, c] = moved[0:H] + moved[D : D + H]
    coef = coef_v[...]
    inverse_coef = 1.0 / coef

    def wide(high, low):
        return jnp.concatenate([high, high, low], axis=0).astype(F32).T.astype(BF16)

    both = dot(to_face, jnp.concatenate(split(lift_v[...]), axis=1))
    w_lift[...] = wide(both[:, :D], both[:, D:])
    th, tl = split(tlift_v[...])
    w_time[...] = wide(th, tl)
    bh, bl = split(binv_v[...])
    w_inv[...] = jnp.concatenate([bh, bh, bl], axis=1)
    both = lax.dot_general(
        jnp.concatenate([th, tl, th], axis=1), w_inv[...], (((1,), (1,)), ((), ())), preferred_element_type=F32
    )
    w_both[...] = wide(*split(both))

    def lateral_jumps(k):
        for g in range(2):
            a, b = 2 + 2 * g, 3 + 2 * g
            for x in range(LAYERS):
                for side, f in ((0, b), (1, a)):
                    high, low = split(work[f * FD : (f + 1) * FD, layer(x)])
                    lat[x * 2 * FD : x * 2 * FD + FD, layer(side)] = high
                    lat[x * 2 * FD + FD : (x + 1) * 2 * FD, layer(side)] = low
            seen = dot(lat[...], lat_maps[g])
            for x in range(LAYERS):
                both = seen[x * 2 * FD : x * 2 * FD + FD] + seen[x * 2 * FD + FD : (x + 1) * 2 * FD]
                for side, f in ((0, a), (1, b)):
                    jumps[k, f * FD : (f + 1) * FD, layer(x)] = work[f * FD : (f + 1) * FD, layer(x)] - both[:, layer(side)]
        for x in range(1, LAYERS):
            jumps[k, 0:FD, layer(x)] = work[0:FD, layer(x)] - work[FD : 2 * FD, layer(x - 1)]
            jumps[k, FD : 2 * FD, layer(x - 1)] = work[FD : 2 * FD, layer(x - 1)] - work[0:FD, layer(x)]

    def rim_jumps(k, copies):
        copies[0].wait_recv()
        copies[1].wait_recv()
        from_lower = jnp.where(p == 0, 0.0, rim_in[k, 0])
        jumps[k, 0:FD, layer(0)] = work[0:FD, layer(0)] - from_lower
        turned = dot(jnp.concatenate(split(rim_in[k, 1]), axis=0), in_map)
        from_upper = jnp.where(p == ns - 1, 0.0, turned[:FD] + turned[FD:])
        last = layer(LAYERS - 1)
        jumps[k, FD : 2 * FD, last] = work[FD : 2 * FD, last] - from_upper

    def apply_local(k):
        jsplit[...] = stack3(jumps[k, 0:R])
        return coef * work[R : R + D, :] + dot(w_lift[...], jsplit[...])

    know(1)
    work[...] = dot(w_vol[...], x3[...])
    lateral_jumps(0)
    loads["rhs"].wait()
    moved = dot(jnp.concatenate(split(rhs_v[...]), axis=0), place[...])
    pre[...] = moved[:D] + moved[D:]
    rim_jumps(0, rims)
    pre[...] = pre[...] - apply_local(0)
    r3[...] = stack3(pre[...])
    bpre[...] = dot(w_inv[...], r3[...]) * inverse_coef

    end_copies[0].wait_recv()
    moved_end[...] = dot(jnp.concatenate(split(end_in[0, :, 0:CUT]), axis=0), place[0:CUT, :])
    end_copies[1].wait_recv()
    late = jnp.concatenate(split(end_in[0, :, CUT:E]), axis=0)
    moved = moved_end[...] + dot(late, place[CUT:E, :])
    jump = start_v[...] - jnp.where(t == 0, 0.0, moved[:H] + moved[H:])
    jumps[0, R:, :] = jump
    t3[...] = stack3(jump)
    dir_copies = {}
    for q in PARTS:
        c = part(q)
        direction = bpre[:, c] - dot(w_both[...], t3[:, c]) * inverse_coef[:, c]
        direc[:, c] = direction
        dir_copies[q] = send_end(1, q, direc, pl.ds(q * W, W))
        x3[:, c] = stack3(direction)
        if q == 3:
            rim_out[1, 1] = dot(w_vol[0:FD, :], x3[:, layer(0)])
            rim = dot(w_vol[FD : 2 * FD, :], x3[:, layer(LAYERS - 1)])
            turned = dot(jnp.concatenate(split(rim), axis=0), out_map)
            rim_out[1, 0] = turned[:FD] + turned[FD:]
            rims2 = send_rims(1)
    know(2)

    work[...] = dot(w_vol[...], x3[...])
    residual = pre[...] - dot(w_time[...], t3[...])
    resid[...] = residual
    rows[2:3, :] = over(residual * residual) + 0.5 * over(jumps[0, :R] * jumps[0, :R]) + over(jumps[0, R:] * jumps[0, R:])
    lateral_jumps(1)
    rim_jumps(1, rims2)
    pre[...] = apply_local(1)
    mixed = over(jumps[0, :R] * jumps[1, :R])
    quad = 0.5 * over(jumps[1, :R] * jumps[1, :R])
    folded = jnp.zeros((8, NB), F32)
    for q in PARTS:
        c = part(q)
        dir_copies[q].wait_recv()
        jump = direc[0:H, c] - jnp.where(t == 0, 0.0, end_in[1, :, c])
        image = pre[:, c] + dot(w_time[...], stack3(jump))
        cross = over(resid[:, c] * image)
        square = over(image * image)
        part_rows = jnp.concatenate(
            [
                cross,
                square,
                rows[2:3, c],
                mixed[:, c] + 2.0 * over(jumps[0, R:, c] * jump) - 2.0 * cross,
                quad[:, c] + square + over(jump * jump),
                jnp.zeros((3, W), F32),
            ],
            axis=0,
        )
        rows[:, c] = part_rows
        folded = folded + part_rows[:, :NB] + part_rows[:, NB:]
    sums = jnp.sum(folded, axis=1, keepdims=True)
    diagonal = iota((8, NB), 0) == iota((8, NB), 1)
    message = jnp.sum(jnp.where(diagonal, sums, 0.0), axis=0, keepdims=True)

    def exchange(buf, me, count, axis, n):
        for d in range(1, count):
            pltpu.make_async_remote_copy(
                src_ref=buf.at[me],
                dst_ref=buf.at[me],
                send_sem=sum_send.at[n],
                recv_sem=sum_recv.at[n],
                device_id={axis: lax.rem(me + d, count)},
                device_id_type=MESH,
            ).start()
        others = buf.at[pl.ds(0, count - 1)]
        return pltpu.make_async_copy(others, others, sum_recv.at[n])

    know(3, (0,))
    row_a[t] = message
    got = exchange(row_a, t, nt, "tm", 0)
    know(3, (1,))
    eh = rows[...].astype(BF16)
    rest = rows[...] - eh.astype(F32)
    em = rest.astype(BF16)
    el = (rest - em.astype(F32)).astype(BF16)
    back = lax.dot_general(
        jnp.concatenate([x3[0 : 2 * D, :], eh, em, el, jnp.zeros((8, E), BF16)], axis=0),
        place[...],
        (((1,), (1,)), ((), ())),
        preferred_element_type=F32,
    )
    dir_o[...] = back[:D] + back[D : 2 * D]
    eta_o[...] = back[2 * D : 2 * D + 8] + back[2 * D + 8 : 2 * D + 16] + back[2 * D + 16 : 2 * D + 24]
    got.wait()
    total = row_a[0]
    for d in range(1, nt):
        total = total + row_a[d]
    know(4, (1,))
    row_b[p] = total
    exchange(row_b, p, ns, "space", 1).wait()
    total = row_b[0]
    for d in range(1, ns):
        total = total + row_b[d]
    tot_o[...] = total

    for copy in end_copies + [dir_copies[q] for q in PARTS] + rims + rims2:
        copy.wait_send()
    for buf, count, n in ((row_a, nt, 0), (row_b, ns, 1)):
        sent = buf.at[pl.ds(0, count - 1)]
        pltpu.make_async_copy(sent, sent, sum_send.at[n]).wait()


def finish(count, init_v, dir_v, eta_v, tot_v, out_o, ind_o, est_o):
    cross, square, base, mixed, quad = (tot_v[0:1, k : k + 1] for k in range(5))
    step = cross / square
    eta_total = base + step * mixed + step * step * quad
    out_o[0] = init_v[0] + step * dir_v[...]
    eta = eta_v[2:3] + step * eta_v[3:4] + step * step * eta_v[4:5]
    ind_o[...] = eta * count / eta_total
    est_o[...] = jnp.broadcast_to(jnp.sqrt(eta_total / count), (1, NB))


def on_device(nt, ns, initial, rhs, coef, stiffness, block_inverse, face_proj, lift, time_lift, neighbour, boundary, send_list):
    vmem = pltpu.VMEM
    hbm_spec = pl.BlockSpec(memory_space=pltpu.HBM)
    vmem_spec = pl.BlockSpec(memory_space=vmem)
    dma = pltpu.SemaphoreType.DMA
    direction, eta, totals = pl.pallas_call(
        functools.partial(kernel, nt, ns),
        out_shape=(
            jax.ShapeDtypeStruct((D, E), F32),
            jax.ShapeDtypeStruct((8, E), F32),
            jax.ShapeDtypeStruct((1, NB), F32),
        ),
        in_specs=[hbm_spec] * 11,
        out_specs=[vmem_spec] * 3,
        scratch_shapes=[
            vmem((D, E), F32),
            vmem((D, E), F32),
            vmem((1, E), F32),
            vmem((D, D), F32),
            vmem((D, D), F32),
            vmem((R, D), F32),
            vmem((R, D), F32),
            vmem((H, D), F32),
            vmem((6, E), jnp.int32),
            vmem((6, E), jnp.int32),
            vmem((2, NB), jnp.int32),
            vmem((E, E), BF16),
            vmem((H, E), F32),
            vmem((2 * D + 16, E), BF16),
            vmem((3 * D, E), BF16),
            vmem((3 * D, E), BF16),
            vmem((3 * H, E), BF16),
            vmem((R + D, E), F32),
            vmem((LAYERS * 2 * FD, 2 * NB), BF16),
            vmem((2, 256, E), F32),
            vmem((3 * R, E), BF16),
            vmem((D, E), F32),
            vmem((D, E), F32),
            vmem((2 * H, E), F32),
            vmem((D, E), F32),
            vmem((D, E), F32),
            vmem((8, E), F32),
            vmem((R + D, 3 * D), BF16),
            vmem((D, 3 * R), BF16),
            vmem((D, 3 * H), BF16),
            vmem((D, 3 * D), BF16),
            vmem((D, 3 * H), BF16),
            vmem((2, 2, FD, NB), F32),
            vmem((2, 2, FD, NB), F32),
            vmem((2, H, E), F32),
            vmem((nt, 1, NB), F32),
            vmem((ns, 1, NB), F32),
            dma((11,)),
            dma((2, 4)),
            dma((2, 4)),
            dma((2, 2)),
            dma((2, 2)),
            dma((2,)),
            dma((2,)),
            pltpu.SemaphoreType.REGULAR((max(1, len(rounds(nt)) + len(rounds(ns))),)),
        ],
        compiler_params=pltpu.CompilerParams(collective_id=0, has_side_effects=True, vmem_limit_bytes=40 * 1024 * 1024),
        cost_estimate=pl.CostEstimate(flops=4 * 10**9, bytes_accessed=3 * 2**20, transcendentals=0),
    )(
        *(
            pltpu.with_memory_space_constraint(x, pltpu.HBM)
            for x in (
                initial,
                rhs,
                coef.reshape(1, E),
                stiffness,
                block_inverse,
                face_proj,
                lift.T,
                time_lift.T,
                neighbour,
                boundary,
                send_list.reshape(2, NB),
            )
        )
    )
    smoothed, indicator, estimate = pl.pallas_call(
        functools.partial(finish, float(E * nt * ns)),
        out_shape=(
            jax.ShapeDtypeStruct((1, D, E), F32),
            jax.ShapeDtypeStruct((1, E), F32),
            jax.ShapeDtypeStruct((1, NB), F32),
        ),
        in_specs=[vmem_spec] * 4,
        out_specs=[vmem_spec] * 3,
        compiler_params=pltpu.CompilerParams(vmem_limit_bytes=8 * 1024 * 1024),
        cost_estimate=pl.CostEstimate(flops=3 * 10**5, bytes_accessed=2**20, transcendentals=0),
    )(initial, direction, eta, totals)
    return smoothed, indicator, estimate[0, :1]


def solution(mesh):
    return jax.shard_map(
        functools.partial(on_device, mesh.shape["tm"], mesh.shape["space"]),
        mesh=mesh,
        in_specs=(
            P("tm", None, "space"),
            P("tm", None, "space"),
            P("space"),
            P(),
            P(),
            P(),
            P(),
            P(),
            P(None, "space"),
            P(None, "space"),
            P("space"),
        ),
        out_specs=(P("tm", None, "space"), P("tm", "space"), P()),
        check_vma=False,
    )
```

```python
import functools

import jax
import jax.numpy as jnp
from jax import lax
from jax.experimental import pallas as pl
from jax.experimental.pallas import tpu as pltpu
from jax.sharding import PartitionSpec as P

MESH = pl.DeviceIdType.MESH
F32 = jnp.float32
BF16 = jnp.bfloat16
D = 128
H = 64
FD = 32
R = 192
LAYERS = 8
NB = 128
E = 1024


def split(x):
    high = x.astype(BF16)
    return high, (x - high.astype(F32)).astype(BF16)


def dot(a, b):
    return jnp.dot(a, b, preferred_element_type=F32)


def iota(shape, dim):
    return lax.broadcasted_iota(jnp.int32, shape, dim)


def one_hot(mask):
    return jnp.where(mask, 1.0, 0.0).astype(BF16)


def column(row):
    eye = iota((NB, NB), 0) == iota((NB, NB), 1)
    return jnp.sum(jnp.where(eye, jnp.broadcast_to(row, (NB, NB)), 0), axis=1, keepdims=True)


def lookup(table, index):
    lane = jnp.broadcast_to(index & 127, (8, NB))
    line = jnp.broadcast_to(index >> 7, (8, NB))
    found = jnp.take_along_axis(table, lane, axis=1)
    return jnp.sum(jnp.where(line == iota((8, NB), 0), found, 0), axis=0, keepdims=True)


def layer(k):
    return slice(k * NB, (k + 1) * NB)


def rounds(n):
    out, known = [], 2
    while known < n // 2:
        out.append(known)
        known *= 2
    return out


def near(n):
    return sorted({1, 2, n - 2, n - 1} & set(range(1, n)))


def stack3(x):
    high, low = split(x)
    return jnp.concatenate([high, low, high], axis=0)


def over(x):
    return jnp.sum(x, axis=0, keepdims=True)


W = 256
SIDES = (slice(0, W), slice(E - W, E))
MIDDLE = slice(W, E - W)
SIDE_LAYERS = (0, 1, 6, 7)
MIDDLE_LAYERS = (2, 3, 4, 5)


def part(q):
    return slice(q * W, (q + 1) * W)


def kernel(
    nt,
    ns,
    init_h,
    rhs_h,
    coef_h,
    stiff_h,
    binv_h,
    fproj_h,
    lift_h,
    tlift_h,
    nbr_h,
    bnd_h,
    send_h,
    dir_o,
    eta_o,
    tot_o,
    init_v,
    rhs_v,
    coef_v,
    weights_v,
    tables_v,
    send_v,
    place,
    start_v,
    xs,
    x3,
    t3,
    work,
    lat,
    jumps,
    pre,
    bpre,
    ends_v,
    resid,
    direc,
    rows,
    w_vol,
    w_lift,
    w_time,
    w_inv,
    w_both,
    w_rim,
    rim_out,
    rim_in,
    end_in,
    row_a,
    row_b,
    load_sem,
    end_send,
    end_recv,
    rim_send,
    rim_recv,
    sum_send,
    sum_recv,
    known_sem,
):
    t = lax.axis_index("tm")
    p = lax.axis_index("space")
    axes = (("tm", t, nt, 0), ("space", p, ns, len(rounds(nt))))

    barrier = pltpu.get_barrier_semaphore()
    for axis, me, n, _ in axes:
        for d in near(n):
            pl.semaphore_signal(barrier, inc=1, device_id={axis: lax.rem(me + d, n)}, device_id_type=MESH)

    def know(k, among=(0, 1)):
        for axis, me, n, base in (axes[i] for i in among):
            reach = rounds(n)
            if 0 < k <= len(reach):
                pl.semaphore_wait(known_sem.at[base + k - 1], 2)
            if k < len(reach):
                for d in (reach[k], n - reach[k]):
                    pl.semaphore_signal(known_sem.at[base + k], inc=1, device_id={axis: lax.rem(me + d, n)}, device_id_type=MESH)

    stiff_v = weights_v.at[pl.ds(0, D)]
    binv_v = weights_v.at[pl.ds(D, D)]
    fproj_v = weights_v.at[pl.ds(2 * D, R)]
    lift_v = weights_v.at[pl.ds(2 * D + R, R)]
    tlift_v = weights_v.at[pl.ds(2 * D + 2 * R, H)]
    nbr_v, bnd_v = tables_v.at[0], tables_v.at[1]
    for n, src, dst in (
        (0, send_h, send_v),
        (1, init_h.at[0], init_v),
        (2, fproj_h, fproj_v),
        (2, stiff_h, stiff_v),
        (2, lift_h, lift_v),
        (2, tlift_h, tlift_v),
        (2, binv_h, binv_v),
        (3, nbr_h, nbr_v),
        (3, bnd_h, bnd_v),
        (4, coef_h, coef_v),
        (5, rhs_h.at[0], rhs_v),
    ):
        pltpu.make_async_copy(src, dst, load_sem.at[n]).start()

    def arrived(ref, sem):
        pltpu.make_async_copy(ref, ref, sem).wait()

    arrived(send_v, load_sem.at[0])
    arrived(init_v, load_sem.at[1])
    arrived(weights_v, load_sem.at[2])
    arrived(tables_v, load_sem.at[3])
    arrived(coef_v, load_sem.at[4])
    up = {"tm": lax.rem(t + 1, nt)}
    upper_part = {"space": lax.rem(p + 1, ns)}
    lower_part = {"space": lax.rem(p + ns - 1, ns)}

    def send_end(k, n, src, columns):
        @pl.when(t < nt - 1)
        def _():
            pltpu.make_async_remote_copy(
                src_ref=src.at[pl.ds(H, H), columns],
                dst_ref=end_in.at[k, :, columns],
                send_sem=end_send.at[0],
                recv_sem=end_recv.at[n],
                device_id=up,
                device_id_type=MESH,
            ).start()

    def end_arrived(ref, n):
        @pl.when(t > 0)
        def _():
            arrived(ref, end_recv.at[n])

    def send_rims(k):
        for side, device, there in ((0, upper_part, p < ns - 1), (1, lower_part, p > 0)):

            @pl.when(there)
            def _():
                pltpu.make_async_remote_copy(
                    src_ref=rim_out.at[k, side],
                    dst_ref=rim_in.at[k, side],
                    send_sem=rim_send.at[side],
                    recv_sem=rim_recv.at[k, side],
                    device_id=device,
                    device_id_type=MESH,
                ).start()

    row, col = iota((R, R), 0), iota((R, R), 1)
    to_face = one_hot(col == (row & 31) * 6 + (row >> 5))
    lower = send_v[0:1, :] & (E - 1)
    upper = send_v[1:2, :] & (E - 1)
    column_ids = iota((E, NB), 0)
    ends = jnp.concatenate([one_hot(column_ids == lower), one_hot(column_ids == upper)], axis=1)
    both = dot(to_face, jnp.concatenate(split(fproj_v[...]), axis=1)).astype(BF16)
    fh, fl = both[:, :D], both[:, D:]
    w_vol[0:R, :] = jnp.concatenate([fh, fh, fl], axis=1)


    def table(ref, f):
        return jnp.concatenate([ref[f : f + 1, layer(k)] for k in range(8)], axis=0)

    first = p == 0
    chain_table = jnp.where(first, table(nbr_v, 0), table(nbr_v, 1)) & (E - 1)
    chain = [jnp.where(first, upper, lower)]
    for k in range(1, LAYERS):
        chain.append(lookup(chain_table, chain[-1]))
    slots = [jnp.where(first, chain[LAYERS - 1 - k], chain[k]) for k in range(LAYERS)]

    ih, il = split(init_v[...])
    xs[0:D, :] = ih
    xs[D : 2 * D, :] = il
    picked = dot(xs[0 : 2 * D, :], ends).astype(BF16)
    rim = dot(w_vol[0 : 2 * FD, :], jnp.concatenate([picked[:D], picked[D:], picked[:D]], axis=0))
    rim_out[0, 1] = rim[0:FD, 0:NB]
    rim_out[0, 0] = rim[FD : 2 * FD, NB : 2 * NB]

    pl.semaphore_wait(barrier, len(near(nt)) + len(near(ns)))
    send_end(0, 0, init_v, pl.ds(0, E))
    send_rims(0)
    know(0)

    base_col = column(slots[0])
    top_col = column(slots[LAYERS - 1])
    out_map = one_hot(top_col == upper)
    in_map = one_hot(column(upper) == slots[LAYERS - 1])
    lateral = []
    for f in range(2, 6):
        target = lookup(table(nbr_v, f) & (E - 1), slots[0])
        wall = lookup(table(bnd_v, f), slots[0])
        lateral.append(one_hot((base_col == target) & (wall == 0)))
    blank = jnp.zeros((NB, NB), BF16)
    lat_maps = [
        jnp.concatenate(
            [
                jnp.concatenate([lateral[2 * g], blank], axis=1),
                jnp.concatenate([blank, lateral[2 * g + 1]], axis=1),
            ],
            axis=0,
        )
        for g in range(2)
    ]

    sh, sl = split(stiff_v[...])
    w_vol[R : R + D, :] = jnp.concatenate([sh, sh, sl], axis=1)

    coef = coef_v[...]
    ch = coef.astype(BF16)
    rest = coef - ch.astype(F32)
    cm = rest.astype(BF16)
    cl = (rest - cm.astype(F32)).astype(BF16)
    xs[2 * D : 2 * D + 16, :] = jnp.concatenate([ch, cm, cl, jnp.zeros((13, E), BF16)], axis=0)
    for q in range(4):
        c = part(q)
        for k in (2 * q, 2 * q + 1):
            place[:, layer(k)] = one_hot(column_ids == slots[k])
        moved = dot(xs[...], place[:, c])
        coef_v[:, c] = moved[2 * D : 2 * D + 1] + moved[2 * D + 1 : 2 * D + 2] + moved[2 * D + 2 : 2 * D + 3]
        xh = moved[0:D].astype(BF16)
        x3[0:D, c] = xh
        x3[D : 2 * D, c] = moved[D : 2 * D].astype(BF16)
        x3[2 * D : 3 * D, c] = xh
        start_v[:, c] = moved[0:H] + moved[D : D + H]
    coef = coef_v[...]
    inverse_coef = 1.0 / coef

    def wide(high, low):
        return jnp.concatenate([high, high, low], axis=0).astype(F32).T.astype(BF16)

    both = dot(to_face, jnp.concatenate(split(lift_v[...]), axis=1))
    w_lift[...] = wide(both[:, :D], both[:, D:])
    lift_high, lift_low = both[:, :D].astype(BF16), both[:, D:].astype(BF16)
    th, tl = split(tlift_v[...])
    w_time[...] = wide(th, tl)
    bh, bl = split(binv_v[...])
    w_inv[...] = jnp.concatenate([bh, bh, bl], axis=1)
    both = lax.dot_general(
        jnp.concatenate([th, tl, th], axis=1), w_inv[...], (((1,), (1,)), ((), ())), preferred_element_type=F32
    )
    w_both[...] = wide(*split(both))
    for f in range(2):
        high, low = lift_high[f * FD : (f + 1) * FD], lift_low[f * FD : (f + 1) * FD]
        both = lax.dot_general(
            jnp.concatenate([high, low, high], axis=1), w_inv[...], (((1,), (1,)), ((), ())), preferred_element_type=F32
        )
        w_rim[f, 0:D, :] = wide(high, low)
        w_rim[f, D : 2 * D, :] = wide(*split(both))

    def lateral_jumps(k, layers):
        count = len(layers) * 2 * FD
        for g in range(2):
            a, b = 2 + 2 * g, 3 + 2 * g
            for n, x in enumerate(layers):
                for side, f in ((0, b), (1, a)):
                    high, low = split(work[f * FD : (f + 1) * FD, layer(x)])
                    lat[n * 2 * FD : n * 2 * FD + FD, layer(side)] = high
                    lat[n * 2 * FD + FD : (n + 1) * 2 * FD, layer(side)] = low
            seen = dot(lat[0:count], lat_maps[g])
            for n, x in enumerate(layers):
                both = seen[n * 2 * FD : n * 2 * FD + FD] + seen[n * 2 * FD + FD : (n + 1) * 2 * FD]
                for side, f in ((0, a), (1, b)):
                    jumps[k, f * FD : (f + 1) * FD, layer(x)] = work[f * FD : (f + 1) * FD, layer(x)] - both[:, layer(side)]
        for x in layers:
            if x > 0:
                jumps[k, 0:FD, layer(x)] = work[0:FD, layer(x)] - work[FD : 2 * FD, layer(x - 1)]
            if x < LAYERS - 1:
                jumps[k, FD : 2 * FD, layer(x)] = work[FD : 2 * FD, layer(x)] - work[0:FD, layer(x + 1)]

    rim_blocks = ((0, layer(0)), (1, layer(LAYERS - 1)))

    def without_rims(k):
        for f, c in rim_blocks:
            jumps[k, f * FD : (f + 1) * FD, c] = jnp.zeros((FD, NB), F32)

    def rims_arrived(k):
        for side, there in ((0, p > 0), (1, p < ns - 1)):

            @pl.when(there)
            def _():
                arrived(rim_in.at[k, side], rim_recv.at[k, side])

    def rim_terms(k):
        turned = dot(jnp.concatenate(split(rim_in[k, 1]), axis=0), in_map)
        outside = (
            jnp.where(p == 0, 0.0, rim_in[k, 0]),
            jnp.where(p == ns - 1, 0.0, turned[:FD] + turned[FD:]),
        )
        found = []
        for f, c in rim_blocks:
            block = work[f * FD : (f + 1) * FD, c] - outside[f]
            jumps[k, f * FD : (f + 1) * FD, c] = block
            added = dot(w_rim[f, 0 : D if k else 2 * D, :], stack3(block))
            found.append((f, c, block, added))
        return found

    def apply_local(k, c):
        return coef[:, c] * work[R : R + D, c] + dot(w_lift[...], stack3(jumps[k, 0:R, c]))

    def move_rhs(c):
        moved = dot(xs[0 : 2 * D, :], place[:, c])
        pre[:, c] = moved[:D] + moved[D:]

    def start_residual(c):
        local = pre[:, c] - apply_local(0, c)
        pre[:, c] = local
        bpre[:, c] = dot(w_inv[...], stack3(local)) * inverse_coef[:, c]

    arrived(rhs_v, load_sem.at[5])
    work[...] = dot(w_vol[...], x3[...])
    rh, rl = split(rhs_v[...])
    xs[0:D, :] = rh
    xs[D : 2 * D, :] = rl
    lateral_jumps(0, SIDE_LAYERS)
    for c in SIDES:
        move_rhs(c)
    without_rims(0)
    for c in SIDES:
        start_residual(c)

    end_arrived(end_in.at[0], 0)
    eh, el = split(end_in[0])
    ends_v[0:H, :] = eh
    ends_v[H : 2 * H, :] = el

    def slab_start(c):
        moved = dot(ends_v[...], place[:, c])
        jump = start_v[:, c] - jnp.where(t == 0, 0.0, moved[:H] + moved[H:])
        jumps[0, R:, c] = jump
        t3[:, c] = stack3(jump)
        direc[:, c] = bpre[:, c] - dot(w_both[...], t3[:, c]) * inverse_coef[:, c]

    for c in SIDES:
        slab_start(c)
    rims_arrived(0)
    know(1)
    for _, c, _, added in rim_terms(0):
        pre[:, c] = pre[:, c] - added[:D]
        direc[:, c] = direc[:, c] - added[D:] * inverse_coef[:, c]
    for c in SIDES:
        x3[:, c] = stack3(direc[:, c])
    for n, c in enumerate(SIDES):
        send_end(1, 1 + n, direc, pl.ds(c.start, W))
    rim_out[1, 1] = dot(w_vol[0:FD, :], x3[:, layer(0)])
    rim = dot(w_vol[FD : 2 * FD, :], x3[:, layer(LAYERS - 1)])
    turned = dot(jnp.concatenate(split(rim), axis=0), out_map)
    rim_out[1, 0] = turned[:FD] + turned[FD:]
    send_rims(1)
    lateral_jumps(0, MIDDLE_LAYERS)
    move_rhs(MIDDLE)
    start_residual(MIDDLE)
    slab_start(MIDDLE)
    x3[:, MIDDLE] = stack3(direc[:, MIDDLE])
    send_end(1, 3, direc, pl.ds(W, E - 2 * W))

    work[...] = dot(w_vol[...], x3[...])
    residual = pre[...] - dot(w_time[...], t3[...])
    resid[...] = residual
    lateral_jumps(1, SIDE_LAYERS + MIDDLE_LAYERS)
    without_rims(1)
    pre[...] = apply_local(1, slice(0, E))
    j0, j1 = jumps[0, :R], jumps[1, :R]
    rows[2:3, :] = over(residual * residual) + 0.5 * over(j0 * j0) + over(jumps[0, R:] * jumps[0, R:])
    rows[3:4, :] = over(j0 * j1)
    rows[4:5, :] = 0.5 * over(j1 * j1)
    rims_arrived(1)
    for f, c, block, added in rim_terms(1):
        pre[:, c] = pre[:, c] + added
        rows[3:4, c] = rows[3:4, c] + over(jumps[0, f * FD : (f + 1) * FD, c] * block)
        rows[4:5, c] = rows[4:5, c] + 0.5 * over(block * block)

    def image_sums(c):
        jump = direc[0:H, c] - jnp.where(t == 0, 0.0, end_in[1, :, c])
        image = pre[:, c] + dot(w_time[...], stack3(jump))
        cross = over(resid[:, c] * image)
        square = over(image * image)
        found = jnp.concatenate(
            [
                cross,
                square,
                rows[2:3, c],
                rows[3:4, c] + 2.0 * over(jumps[0, R:, c] * jump) - 2.0 * cross,
                rows[4:5, c] + square + over(jump * jump),
                jnp.zeros((3, c.stop - c.start), F32),
            ],
            axis=0,
        )
        rows[:, c] = found
        return sum(found[:, layer(k)] for k in range((c.stop - c.start) // NB))

    for n, c in enumerate(SIDES):
        end_arrived(end_in.at[1, :, pl.ds(c.start, W)], 1 + n)
    folded = image_sums(SIDES[0]) + image_sums(SIDES[1])
    end_arrived(end_in.at[1, :, pl.ds(W, E - 2 * W)], 3)
    folded = folded + image_sums(MIDDLE)
    sums = jnp.sum(folded, axis=1, keepdims=True)
    diagonal = iota((8, NB), 0) == iota((8, NB), 1)
    message = jnp.sum(jnp.where(diagonal, sums, 0.0), axis=0, keepdims=True)

    def exchange(buf, me, count, axis, n):
        for d in range(1, count):
            pltpu.make_async_remote_copy(
                src_ref=buf.at[me],
                dst_ref=buf.at[me],
                send_sem=sum_send.at[0],
                recv_sem=sum_recv.at[n],
                device_id={axis: lax.rem(me + d, count)},
                device_id_type=MESH,
            ).start()
        others = buf.at[pl.ds(0, count - 1)]
        return pltpu.make_async_copy(others, others, sum_recv.at[n])

    know(2, (0,))
    row_a[t] = message
    got = exchange(row_a, t, nt, "tm", 0)
    know(2, (1,))
    eh = rows[...].astype(BF16)
    rest = rows[...] - eh.astype(F32)
    em = rest.astype(BF16)
    el = (rest - em.astype(F32)).astype(BF16)
    back = lax.dot_general(
        jnp.concatenate([x3[0 : 2 * D, :], eh, em, el, jnp.zeros((8, E), BF16)], axis=0),
        place[...],
        (((1,), (1,)), ((), ())),
        preferred_element_type=F32,
    )
    dir_o[...] = back[:D] + back[D : 2 * D]
    eta_o[...] = back[2 * D : 2 * D + 8] + back[2 * D + 8 : 2 * D + 16] + back[2 * D + 16 : 2 * D + 24]
    got.wait()
    total = row_a[0]
    for d in range(1, nt):
        total = total + row_a[d]
    know(3, (1,))
    row_b[p] = total
    exchange(row_b, p, ns, "space", 1).wait()
    total = row_b[0]
    for d in range(1, ns):
        total = total + row_b[d]
    tot_o[...] = total

    @pl.when(t < nt - 1)
    def _():
        arrived(end_in, end_send.at[0])

    for side, there in ((0, p < ns - 1), (1, p > 0)):

        @pl.when(there)
        def _():
            arrived(rim_in.at[:, side], rim_send.at[side])

    arrived(row_b.at[pl.ds(0, nt + ns - 2)], sum_send.at[0])


def finish(count, init_v, dir_v, eta_v, tot_v, out_o, ind_o, est_o):
    cross, square, base, mixed, quad = (tot_v[0:1, k : k + 1] for k in range(5))
    step = cross / square
    eta_total = base + step * mixed + step * step * quad
    out_o[0] = init_v[0] + step * dir_v[...]
    eta = eta_v[2:3] + step * eta_v[3:4] + step * step * eta_v[4:5]
    ind_o[...] = eta * count / eta_total
    est_o[...] = jnp.broadcast_to(jnp.sqrt(eta_total / count), (1, NB))


def on_device(nt, ns, initial, rhs, coef, stiffness, block_inverse, face_proj, lift, time_lift, neighbour, boundary, send_list):
    vmem = pltpu.VMEM
    hbm_spec = pl.BlockSpec(memory_space=pltpu.HBM)
    vmem_spec = pl.BlockSpec(memory_space=vmem)
    dma = pltpu.SemaphoreType.DMA
    direction, eta, totals = pl.pallas_call(
        functools.partial(kernel, nt, ns),
        out_shape=(
            jax.ShapeDtypeStruct((D, E), F32),
            jax.ShapeDtypeStruct((8, E), F32),
            jax.ShapeDtypeStruct((1, NB), F32),
        ),
        in_specs=[hbm_spec] * 11,
        out_specs=[vmem_spec] * 3,
        scratch_shapes=[
            vmem((D, E), F32),
            vmem((D, E), F32),
            vmem((1, E), F32),
            vmem((2 * D + 2 * R + H, D), F32),
            vmem((2, 6, E), jnp.int32),
            vmem((2, NB), jnp.int32),
            vmem((E, E), BF16),
            vmem((H, E), F32),
            vmem((2 * D + 16, E), BF16),
            vmem((3 * D, E), BF16),
            vmem((3 * H, E), BF16),
            vmem((R + D, E), F32),
            vmem((LAYERS * 2 * FD, 2 * NB), BF16),
            vmem((2, 256, E), F32),
            vmem((D, E), F32),
            vmem((D, E), F32),
            vmem((2 * H, E), BF16),
            vmem((D, E), F32),
            vmem((D, E), F32),
            vmem((8, E), F32),
            vmem((R + D, 3 * D), BF16),
            vmem((D, 3 * R), BF16),
            vmem((D, 3 * H), BF16),
            vmem((D, 3 * D), BF16),
            vmem((D, 3 * H), BF16),
            vmem((2, 2 * D, 3 * FD), BF16),
            vmem((2, 2, FD, NB), F32),
            vmem((2, 2, FD, NB), F32),
            vmem((2, H, E), F32),
            vmem((nt, 1, NB), F32),
            vmem((nt + ns, 1, NB), F32),
            dma((6,)),
            dma((1,)),
            dma((4,)),
            dma((2,)),
            dma((2, 2)),
            dma((1,)),
            dma((2,)),
            pltpu.SemaphoreType.REGULAR((max(1, len(rounds(nt)) + len(rounds(ns))),)),
        ],
        compiler_params=pltpu.CompilerParams(collective_id=0, has_side_effects=True, vmem_limit_bytes=40 * 1024 * 1024),
        cost_estimate=pl.CostEstimate(flops=4 * 10**9, bytes_accessed=3 * 2**20, transcendentals=0),
    )(
        *(
            pltpu.with_memory_space_constraint(x, pltpu.HBM)
            for x in (
                initial,
                rhs,
                coef.reshape(1, E),
                stiffness,
                block_inverse,
                face_proj,
                lift.T,
                time_lift.T,
                neighbour,
                boundary,
                send_list.reshape(2, NB),
            )
        )
    )
    smoothed, indicator, estimate = pl.pallas_call(
        functools.partial(finish, float(E * nt * ns)),
        out_shape=(
            jax.ShapeDtypeStruct((1, D, E), F32),
            jax.ShapeDtypeStruct((1, E), F32),
            jax.ShapeDtypeStruct((1, NB), F32),
        ),
        in_specs=[vmem_spec] * 4,
        out_specs=[vmem_spec] * 3,
        compiler_params=pltpu.CompilerParams(vmem_limit_bytes=8 * 1024 * 1024),
        cost_estimate=pl.CostEstimate(flops=3 * 10**5, bytes_accessed=2**20, transcendentals=0),
    )(initial, direction, eta, totals)
    return smoothed, indicator, estimate[0, :1]


def solution(mesh):
    return jax.shard_map(
        functools.partial(on_device, mesh.shape["tm"], mesh.shape["space"]),
        mesh=mesh,
        in_specs=(
            P("tm", None, "space"),
            P("tm", None, "space"),
            P("space"),
            P(),
            P(),
            P(),
            P(),
            P(),
            P(None, "space"),
            P(None, "space"),
            P("space"),
        ),
        out_specs=(P("tm", None, "space"), P("tm", "space"), P()),
        check_vma=False,
    )
```

```python
import functools

import jax
import jax.numpy as jnp
from jax import lax
from jax.experimental import pallas as pl
from jax.experimental.pallas import tpu as pltpu
from jax.sharding import PartitionSpec as P

MESH = pl.DeviceIdType.MESH
F32 = jnp.float32
BF16 = jnp.bfloat16
D = 128
H = 64
FD = 32
R = 192
LAYERS = 8
NB = 128
E = 1024


def split(x):
    high = x.astype(BF16)
    return high, (x - high.astype(F32)).astype(BF16)


def dot(a, b):
    return jnp.dot(a, b, preferred_element_type=F32)


def iota(shape, dim):
    return lax.broadcasted_iota(jnp.int32, shape, dim)


def one_hot(mask):
    return jnp.where(mask, 1.0, 0.0).astype(BF16)


def column(row):
    eye = iota((NB, NB), 0) == iota((NB, NB), 1)
    return jnp.sum(jnp.where(eye, jnp.broadcast_to(row, (NB, NB)), 0), axis=1, keepdims=True)


def lookup(table, index):
    lane = jnp.broadcast_to(index & 127, (8, NB))
    line = jnp.broadcast_to(index >> 7, (8, NB))
    found = jnp.take_along_axis(table, lane, axis=1)
    return jnp.sum(jnp.where(line == iota((8, NB), 0), found, 0), axis=0, keepdims=True)


def layer(k):
    return slice(k * NB, (k + 1) * NB)


def rounds(n, known):
    out = []
    while known < n // 2:
        out.append(known)
        known *= 2
    return out


def near(n, radius):
    return [d for d in range(1, n) if min(d, n - d) <= radius]


TM_RADIUS, SPACE_RADIUS = 2, 1
CUT = 768
OUT_PARTS = 2


def stack3(x):
    high, low = split(x)
    return jnp.concatenate([high, low, high], axis=0)


def over(x):
    return jnp.sum(x, axis=0, keepdims=True)


W = 256
SIDES = (slice(0, W), slice(E - W, E))
MIDDLE = slice(W, E - W)
SIDE_LAYERS = (0, 1, 6, 7)
MIDDLE_LAYERS = (2, 3, 4, 5)


def part(q):
    return slice(q * W, (q + 1) * W)


def kernel(
    nt,
    ns,
    init_h,
    rhs_h,
    coef_h,
    stiff_h,
    binv_h,
    fproj_h,
    lift_h,
    tlift_h,
    nbr_h,
    bnd_h,
    send_h,
    init_v,
    dir_o,
    eta_o,
    tot_o,
    rhs_v,
    coef_v,
    weights_v,
    tables_v,
    send_v,
    place,
    start_v,
    xs,
    x3,
    t3,
    work,
    lat,
    jumps,
    pre,
    bpre,
    ends_v,
    moved_v,
    folded_v,
    resid,
    direc,
    rows,
    w_vol,
    w_lift,
    w_time,
    w_inv,
    w_both,
    w_rim,
    rim_out,
    rim_in,
    end_in,
    row_a,
    row_b,
    load_sem,
    end_send,
    end_recv,
    rim_send,
    rim_recv,
    sum_send,
    sum_recv,
    known_sem,
):
    t = lax.axis_index("tm")
    p = lax.axis_index("space")
    tm_rounds, space_rounds = rounds(nt, TM_RADIUS), rounds(ns, SPACE_RADIUS)
    tm_near, space_near = near(nt, TM_RADIUS), near(ns, SPACE_RADIUS)

    barrier = pltpu.get_barrier_semaphore()
    for axis, me, n, close in (("tm", t, nt, tm_near), ("space", p, ns, space_near)):
        for d in close:
            pl.semaphore_signal(barrier, inc=1, device_id={axis: lax.rem(me + d, n)}, device_id_type=MESH)

    def know(axis, k):
        me, n, reach, base = (t, nt, tm_rounds, 0) if axis == "tm" else (p, ns, space_rounds, len(tm_rounds))
        if 0 < k <= len(reach):
            pl.semaphore_wait(known_sem.at[base + k - 1], 2)
        if k < len(reach):
            for d in (reach[k], n - reach[k]):
                pl.semaphore_signal(known_sem.at[base + k], inc=1, device_id={axis: lax.rem(me + d, n)}, device_id_type=MESH)

    stiff_v = weights_v.at[pl.ds(0, D)]
    binv_v = weights_v.at[pl.ds(D, D)]
    fproj_v = weights_v.at[pl.ds(2 * D, R)]
    lift_v = weights_v.at[pl.ds(2 * D + R, R)]
    tlift_v = weights_v.at[pl.ds(2 * D + 2 * R, H)]
    nbr_v, bnd_v = tables_v.at[0], tables_v.at[1]
    for n, src, dst in (
        (0, send_h, send_v),
        (1, init_h.at[0], init_v),
        (2, fproj_h, fproj_v),
        (2, stiff_h, stiff_v),
        (2, lift_h, lift_v),
        (2, tlift_h, tlift_v),
        (2, binv_h, binv_v),
        (3, nbr_h, nbr_v),
        (3, bnd_h, bnd_v),
        (4, coef_h, coef_v),
        (5, rhs_h.at[0], rhs_v),
    ):
        pltpu.make_async_copy(src, dst, load_sem.at[n]).start()

    def arrived(ref, sem):
        pltpu.make_async_copy(ref, ref, sem).wait()

    arrived(send_v, load_sem.at[0])
    arrived(init_v, load_sem.at[1])
    arrived(weights_v, load_sem.at[2])
    arrived(tables_v, load_sem.at[3])
    arrived(coef_v, load_sem.at[4])
    up = {"tm": lax.rem(t + 1, nt)}
    upper_part = {"space": lax.rem(p + 1, ns)}
    lower_part = {"space": lax.rem(p + ns - 1, ns)}

    def send_end(k, n, src, columns):
        @pl.when(t < nt - 1)
        def _():
            pltpu.make_async_remote_copy(
                src_ref=src.at[pl.ds(H, H), columns],
                dst_ref=end_in.at[k, :, columns],
                send_sem=end_send.at[0],
                recv_sem=end_recv.at[n],
                device_id=up,
                device_id_type=MESH,
            ).start()

    def end_arrived(ref, n):
        @pl.when(t > 0)
        def _():
            arrived(ref, end_recv.at[n])

    def send_rims(k):
        for side, device, there in ((0, upper_part, p < ns - 1), (1, lower_part, p > 0)):

            @pl.when(there)
            def _():
                pltpu.make_async_remote_copy(
                    src_ref=rim_out.at[k, side],
                    dst_ref=rim_in.at[k, side],
                    send_sem=rim_send.at[side],
                    recv_sem=rim_recv.at[k, side],
                    device_id=device,
                    device_id_type=MESH,
                ).start()

    pl.semaphore_wait(barrier, len(tm_near) + len(space_near))
    send_end(0, 0, init_v, pl.ds(0, CUT))
    send_end(0, 4, init_v, pl.ds(CUT, E - CUT))

    row, col = iota((R, R), 0), iota((R, R), 1)
    to_face = one_hot(col == (row & 31) * 6 + (row >> 5))
    lower = send_v[0:1, :] & (E - 1)
    upper = send_v[1:2, :] & (E - 1)
    column_ids = iota((E, NB), 0)
    ends = jnp.concatenate([one_hot(column_ids == lower), one_hot(column_ids == upper)], axis=1)
    both = dot(to_face, jnp.concatenate(split(fproj_v[...]), axis=1)).astype(BF16)
    fh, fl = both[:, :D], both[:, D:]
    w_vol[0:R, :] = jnp.concatenate([fh, fh, fl], axis=1)


    def table(ref, f):
        return jnp.concatenate([ref[f : f + 1, layer(k)] for k in range(8)], axis=0)

    first = p == 0
    chain_table = jnp.where(first, table(nbr_v, 0), table(nbr_v, 1)) & (E - 1)
    chain = [jnp.where(first, upper, lower)]
    for k in range(1, LAYERS):
        chain.append(lookup(chain_table, chain[-1]))
    slots = [jnp.where(first, chain[LAYERS - 1 - k], chain[k]) for k in range(LAYERS)]

    ih, il = split(init_v[...])
    xs[0:D, :] = ih
    xs[D : 2 * D, :] = il
    picked = dot(xs[0 : 2 * D, :], ends).astype(BF16)
    rim = dot(w_vol[0 : 2 * FD, :], jnp.concatenate([picked[:D], picked[D:], picked[:D]], axis=0))
    rim_out[0, 1] = rim[0:FD, 0:NB]
    rim_out[0, 0] = rim[FD : 2 * FD, NB : 2 * NB]

    send_rims(0)
    know("tm", 0)
    know("space", 0)

    base_col = column(slots[0])
    top_col = column(slots[LAYERS - 1])
    out_map = one_hot(top_col == upper)
    in_map = one_hot(column(upper) == slots[LAYERS - 1])
    lateral = []
    for f in range(2, 6):
        target = lookup(table(nbr_v, f) & (E - 1), slots[0])
        wall = lookup(table(bnd_v, f), slots[0])
        lateral.append(one_hot((base_col == target) & (wall == 0)))
    blank = jnp.zeros((NB, NB), BF16)
    lat_maps = [
        jnp.concatenate(
            [
                jnp.concatenate([lateral[2 * g], blank], axis=1),
                jnp.concatenate([blank, lateral[2 * g + 1]], axis=1),
            ],
            axis=0,
        )
        for g in range(2)
    ]

    sh, sl = split(stiff_v[...])
    w_vol[R : R + D, :] = jnp.concatenate([sh, sh, sl], axis=1)

    coef = coef_v[...]
    ch = coef.astype(BF16)
    rest = coef - ch.astype(F32)
    cm = rest.astype(BF16)
    cl = (rest - cm.astype(F32)).astype(BF16)
    xs[2 * D : 2 * D + 16, :] = jnp.concatenate([ch, cm, cl, jnp.zeros((13, E), BF16)], axis=0)
    for q in range(4):
        c = part(q)
        for k in (2 * q, 2 * q + 1):
            place[:, layer(k)] = one_hot(column_ids == slots[k])
        moved = dot(xs[...], place[:, c])
        coef_v[:, c] = moved[2 * D : 2 * D + 1] + moved[2 * D + 1 : 2 * D + 2] + moved[2 * D + 2 : 2 * D + 3]
        xh = moved[0:D].astype(BF16)
        x3[0:D, c] = xh
        x3[D : 2 * D, c] = moved[D : 2 * D].astype(BF16)
        x3[2 * D : 3 * D, c] = xh
        start_v[:, c] = moved[0:H] + moved[D : D + H]
    coef = coef_v[...]
    inverse_coef = 1.0 / coef

    def wide(high, low):
        return jnp.concatenate([high, high, low], axis=0).astype(F32).T.astype(BF16)

    both = dot(to_face, jnp.concatenate(split(lift_v[...]), axis=1))
    w_lift[...] = wide(both[:, :D], both[:, D:])
    lift_high, lift_low = both[:, :D].astype(BF16), both[:, D:].astype(BF16)
    th, tl = split(tlift_v[...])
    w_time[...] = wide(th, tl)
    bh, bl = split(binv_v[...])
    w_inv[...] = jnp.concatenate([bh, bh, bl], axis=1)
    both = lax.dot_general(
        jnp.concatenate([th, tl, th], axis=1), w_inv[...], (((1,), (1,)), ((), ())), preferred_element_type=F32
    )
    w_both[...] = wide(*split(both))
    for f in range(2):
        high, low = lift_high[f * FD : (f + 1) * FD], lift_low[f * FD : (f + 1) * FD]
        both = lax.dot_general(
            jnp.concatenate([high, low, high], axis=1), w_inv[...], (((1,), (1,)), ((), ())), preferred_element_type=F32
        )
        w_rim[f, 0:D, :] = wide(high, low)
        w_rim[f, D : 2 * D, :] = wide(*split(both))

    def lateral_jumps(k, layers):
        count = len(layers) * 2 * FD
        for g in range(2):
            a, b = 2 + 2 * g, 3 + 2 * g
            for n, x in enumerate(layers):
                for side, f in ((0, b), (1, a)):
                    high, low = split(work[f * FD : (f + 1) * FD, layer(x)])
                    lat[n * 2 * FD : n * 2 * FD + FD, layer(side)] = high
                    lat[n * 2 * FD + FD : (n + 1) * 2 * FD, layer(side)] = low
            seen = dot(lat[0:count], lat_maps[g])
            for n, x in enumerate(layers):
                both = seen[n * 2 * FD : n * 2 * FD + FD] + seen[n * 2 * FD + FD : (n + 1) * 2 * FD]
                for side, f in ((0, a), (1, b)):
                    jumps[k, f * FD : (f + 1) * FD, layer(x)] = work[f * FD : (f + 1) * FD, layer(x)] - both[:, layer(side)]
        for x in layers:
            if x > 0:
                jumps[k, 0:FD, layer(x)] = work[0:FD, layer(x)] - work[FD : 2 * FD, layer(x - 1)]
            if x < LAYERS - 1:
                jumps[k, FD : 2 * FD, layer(x)] = work[FD : 2 * FD, layer(x)] - work[0:FD, layer(x + 1)]

    rim_blocks = ((0, layer(0)), (1, layer(LAYERS - 1)))

    def without_rims(k):
        for f, c in rim_blocks:
            jumps[k, f * FD : (f + 1) * FD, c] = jnp.zeros((FD, NB), F32)

    def rims_arrived(k):
        for side, there in ((0, p > 0), (1, p < ns - 1)):

            @pl.when(there)
            def _():
                arrived(rim_in.at[k, side], rim_recv.at[k, side])

    def rim_terms(k):
        turned = dot(jnp.concatenate(split(rim_in[k, 1]), axis=0), in_map)
        outside = (
            jnp.where(p == 0, 0.0, rim_in[k, 0]),
            jnp.where(p == ns - 1, 0.0, turned[:FD] + turned[FD:]),
        )
        found = []
        for f, c in rim_blocks:
            block = work[f * FD : (f + 1) * FD, c] - outside[f]
            jumps[k, f * FD : (f + 1) * FD, c] = block
            added = dot(w_rim[f, 0 : D if k else 2 * D, :], stack3(block))
            found.append((f, c, block, added))
        return found

    def apply_local(k, c):
        return coef[:, c] * work[R : R + D, c] + dot(w_lift[...], stack3(jumps[k, 0:R, c]))

    def move_rhs(c):
        moved = dot(xs[0 : 2 * D, :], place[:, c])
        pre[:, c] = moved[:D] + moved[D:]

    def start_residual(c):
        local = pre[:, c] - apply_local(0, c)
        pre[:, c] = local
        bpre[:, c] = dot(w_inv[...], stack3(local)) * inverse_coef[:, c]

    arrived(rhs_v, load_sem.at[5])
    work[...] = dot(w_vol[...], x3[...])
    rh, rl = split(rhs_v[...])
    xs[0:D, :] = rh
    xs[D : 2 * D, :] = rl
    lateral_jumps(0, SIDE_LAYERS)
    for c in SIDES:
        move_rhs(c)
    without_rims(0)
    for c in SIDES:
        start_residual(c)

    know("tm", 1)
    know("space", 1)
    def take_ends(first, last):
        eh, el = split(end_in[0, :, first:last])
        ends_v[0:H, first:last] = eh
        ends_v[H : 2 * H, first:last] = el

    end_arrived(end_in.at[0, :, pl.ds(0, CUT)], 0)
    take_ends(0, CUT)
    for c in SIDES:
        moved_v[:, c] = dot(ends_v[:, 0:CUT], place[0:CUT, c])
    end_arrived(end_in.at[0, :, pl.ds(CUT, E - CUT)], 4)
    take_ends(CUT, E)
    for c in SIDES:
        moved_v[:, c] = moved_v[:, c] + dot(ends_v[:, CUT:E], place[CUT:E, c])

    def slab_start(c):
        moved = moved_v[:, c]
        jump = start_v[:, c] - jnp.where(t == 0, 0.0, moved[:H] + moved[H:])
        jumps[0, R:, c] = jump
        t3[:, c] = stack3(jump)
        direc[:, c] = bpre[:, c] - dot(w_both[...], t3[:, c]) * inverse_coef[:, c]

    for c in SIDES:
        slab_start(c)
    rims_arrived(0)
    for _, c, _, added in rim_terms(0):
        pre[:, c] = pre[:, c] - added[:D]
        direc[:, c] = direc[:, c] - added[D:] * inverse_coef[:, c]
    for c in SIDES:
        x3[:, c] = stack3(direc[:, c])
    for n, c in enumerate(SIDES):
        send_end(1, 1 + n, direc, pl.ds(c.start, W))
    rim_out[1, 1] = dot(w_vol[0:FD, :], x3[:, layer(0)])
    rim = dot(w_vol[FD : 2 * FD, :], x3[:, layer(LAYERS - 1)])
    turned = dot(jnp.concatenate(split(rim), axis=0), out_map)
    rim_out[1, 0] = turned[:FD] + turned[FD:]
    send_rims(1)
    lateral_jumps(0, MIDDLE_LAYERS)
    move_rhs(MIDDLE)
    start_residual(MIDDLE)
    moved_v[:, MIDDLE] = dot(ends_v[...], place[:, MIDDLE])
    slab_start(MIDDLE)
    x3[:, MIDDLE] = stack3(direc[:, MIDDLE])
    send_end(1, 3, direc, pl.ds(W, E - 2 * W))
    know("space", 2)

    work[...] = dot(w_vol[...], x3[...])
    residual = pre[...] - dot(w_time[...], t3[...])
    resid[...] = residual
    lateral_jumps(1, SIDE_LAYERS + MIDDLE_LAYERS)
    without_rims(1)
    pre[...] = apply_local(1, slice(0, E))
    j0, j1 = jumps[0, :R], jumps[1, :R]
    rows[2:3, :] = over(residual * residual) + 0.5 * over(j0 * j0) + over(jumps[0, R:] * jumps[0, R:])
    rows[3:4, :] = over(j0 * j1)
    rows[4:5, :] = 0.5 * over(j1 * j1)
    def image_sums(c):
        jump = direc[0:H, c] - jnp.where(t == 0, 0.0, end_in[1, :, c])
        image = pre[:, c] + dot(w_time[...], stack3(jump))
        cross = over(resid[:, c] * image)
        square = over(image * image)
        found = jnp.concatenate(
            [
                cross,
                square,
                rows[2:3, c],
                rows[3:4, c] + 2.0 * over(jumps[0, R:, c] * jump) - 2.0 * cross,
                rows[4:5, c] + square + over(jump * jump),
                jnp.zeros((3, c.stop - c.start), F32),
            ],
            axis=0,
        )
        rows[:, c] = found
        return sum(found[:, layer(k)] for k in range((c.stop - c.start) // NB))

    def middle_sums():
        end_arrived(end_in.at[1, :, pl.ds(W, E - 2 * W)], 3)
        folded_v[...] = image_sums(MIDDLE)

    rims_last = lax.rem(p, LAYERS) == 0

    @pl.when(rims_last)
    def _():
        middle_sums()

    for n, c in enumerate(SIDES):
        end_arrived(end_in.at[1, :, pl.ds(c.start, W)], 1 + n)
    rims_arrived(1)
    for f, c, block, added in rim_terms(1):
        pre[:, c] = pre[:, c] + added
        rows[3:4, c] = rows[3:4, c] + over(jumps[0, f * FD : (f + 1) * FD, c] * block)
        rows[4:5, c] = rows[4:5, c] + 0.5 * over(block * block)

    folded = image_sums(SIDES[0]) + image_sums(SIDES[1])

    @pl.when(jnp.logical_not(rims_last))
    def _():
        middle_sums()

    folded = folded + folded_v[...]
    sums = jnp.sum(folded, axis=1, keepdims=True)
    diagonal = iota((8, NB), 0) == iota((8, NB), 1)
    message = jnp.sum(jnp.where(diagonal, sums, 0.0), axis=0, keepdims=True)

    def exchange(buf, me, count, axis, n):
        for d in range(1, count):
            pltpu.make_async_remote_copy(
                src_ref=buf.at[me],
                dst_ref=buf.at[me],
                send_sem=sum_send.at[0],
                recv_sem=sum_recv.at[n],
                device_id={axis: lax.rem(me + d, count)},
                device_id_type=MESH,
            ).start()
        others = buf.at[pl.ds(0, count - 1)]
        return pltpu.make_async_copy(others, others, sum_recv.at[n])

    know("tm", 2)
    row_a[t] = message
    got = exchange(row_a, t, nt, "tm", 0)
    eh = rows[...].astype(BF16)
    rest = rows[...] - eh.astype(F32)
    em = rest.astype(BF16)
    el = (rest - em.astype(F32)).astype(BF16)
    back = lax.dot_general(
        jnp.concatenate([x3[0 : 2 * D, :], eh, em, el, jnp.zeros((8, E), BF16)], axis=0),
        place[...],
        (((1,), (1,)), ((), ())),
        preferred_element_type=F32,
    )
    dir_o[...] = back[:D] + back[D : 2 * D]
    eta_o[...] = back[2 * D : 2 * D + 8] + back[2 * D + 8 : 2 * D + 16] + back[2 * D + 16 : 2 * D + 24]
    know("space", 3)
    got.wait()
    total = row_a[0]
    for d in range(1, nt):
        total = total + row_a[d]
    know("space", 4)
    row_b[p] = total
    exchange(row_b, p, ns, "space", 1).wait()
    total = row_b[0]
    for d in range(1, ns):
        total = total + row_b[d]
    tot_o[...] = total

    @pl.when(t < nt - 1)
    def _():
        arrived(end_in, end_send.at[0])

    for side, there in ((0, p < ns - 1), (1, p > 0)):

        @pl.when(there)
        def _():
            arrived(rim_in.at[:, side], rim_send.at[side])

    arrived(row_b.at[pl.ds(0, nt + ns - 2)], sum_send.at[0])


def finish(count, init_v, dir_v, eta_v, tot_v, out_h, ind_h, est_h, out_v, ind_v, est_v, sem):
    cross, square, base, mixed, quad = (tot_v[0:1, k : k + 1] for k in range(5))
    step = cross / square
    copies = []

    def send(src, dst):
        copies.append(pltpu.make_async_copy(src, dst, sem.at[len(copies)]))
        copies[-1].start()

    for k in range(OUT_PARTS):
        part_rows = pl.ds(k * (D // OUT_PARTS), D // OUT_PARTS)
        out_v[part_rows] = init_v[part_rows] + step * dir_v[part_rows]
        send(out_v.at[part_rows], out_h.at[0, part_rows])
    eta_total = base + step * mixed + step * step * quad
    eta = eta_v[2:3] + step * eta_v[3:4] + step * step * eta_v[4:5]
    ind_v[...] = eta * count / eta_total
    send(ind_v, ind_h)
    est_v[...] = jnp.broadcast_to(jnp.sqrt(eta_total / count), (1, NB))
    send(est_v, est_h)
    for copy in copies:
        copy.wait()


def on_device(nt, ns, initial, rhs, coef, stiffness, block_inverse, face_proj, lift, time_lift, neighbour, boundary, send_list):
    vmem = pltpu.VMEM
    hbm_spec = pl.BlockSpec(memory_space=pltpu.HBM)
    vmem_spec = pl.BlockSpec(memory_space=vmem)
    dma = pltpu.SemaphoreType.DMA
    iterate, direction, eta, totals = pl.pallas_call(
        functools.partial(kernel, nt, ns),
        out_shape=(
            jax.ShapeDtypeStruct((D, E), F32),
            jax.ShapeDtypeStruct((D, E), F32),
            jax.ShapeDtypeStruct((8, E), F32),
            jax.ShapeDtypeStruct((1, NB), F32),
        ),
        in_specs=[hbm_spec] * 11,
        out_specs=[vmem_spec] * 4,
        scratch_shapes=[
            vmem((D, E), F32),
            vmem((1, E), F32),
            vmem((2 * D + 2 * R + H, D), F32),
            vmem((2, 6, E), jnp.int32),
            vmem((2, NB), jnp.int32),
            vmem((E, E), BF16),
            vmem((H, E), F32),
            vmem((2 * D + 16, E), BF16),
            vmem((3 * D, E), BF16),
            vmem((3 * H, E), BF16),
            vmem((R + D, E), F32),
            vmem((LAYERS * 2 * FD, 2 * NB), BF16),
            vmem((2, 256, E), F32),
            vmem((D, E), F32),
            vmem((D, E), F32),
            vmem((2 * H, E), BF16),
            vmem((2 * H, E), F32),
            vmem((8, NB), F32),
            vmem((D, E), F32),
            vmem((D, E), F32),
            vmem((8, E), F32),
            vmem((R + D, 3 * D), BF16),
            vmem((D, 3 * R), BF16),
            vmem((D, 3 * H), BF16),
            vmem((D, 3 * D), BF16),
            vmem((D, 3 * H), BF16),
            vmem((2, 2 * D, 3 * FD), BF16),
            vmem((2, 2, FD, NB), F32),
            vmem((2, 2, FD, NB), F32),
            vmem((2, H, E), F32),
            vmem((nt, 1, NB), F32),
            vmem((nt + ns, 1, NB), F32),
            dma((6,)),
            dma((1,)),
            dma((5,)),
            dma((2,)),
            dma((2, 2)),
            dma((1,)),
            dma((2,)),
            pltpu.SemaphoreType.REGULAR((max(1, len(rounds(nt, TM_RADIUS)) + len(rounds(ns, SPACE_RADIUS))),)),
        ],
        compiler_params=pltpu.CompilerParams(collective_id=0, has_side_effects=True, vmem_limit_bytes=40 * 1024 * 1024),
        cost_estimate=pl.CostEstimate(flops=4 * 10**9, bytes_accessed=3 * 2**20, transcendentals=0),
    )(
        *(
            pltpu.with_memory_space_constraint(x, pltpu.HBM)
            for x in (
                initial,
                rhs,
                coef.reshape(1, E),
                stiffness,
                block_inverse,
                face_proj,
                lift.T,
                time_lift.T,
                neighbour,
                boundary,
                send_list.reshape(2, NB),
            )
        )
    )
    smoothed, indicator, estimate = pl.pallas_call(
        functools.partial(finish, float(E * nt * ns)),
        out_shape=(
            jax.ShapeDtypeStruct((1, D, E), F32),
            jax.ShapeDtypeStruct((1, E), F32),
            jax.ShapeDtypeStruct((1, NB), F32),
        ),
        in_specs=[vmem_spec] * 4,
        out_specs=[hbm_spec] * 3,
        scratch_shapes=[
            vmem((D, E), F32),
            vmem((1, E), F32),
            vmem((1, NB), F32),
            dma((OUT_PARTS + 2,)),
        ],
        compiler_params=pltpu.CompilerParams(vmem_limit_bytes=8 * 1024 * 1024),
        cost_estimate=pl.CostEstimate(flops=3 * 10**5, bytes_accessed=2**20, transcendentals=0),
    )(iterate, direction, eta, totals)
    return smoothed, indicator, estimate[0, :1]


def solution(mesh):
    return jax.shard_map(
        functools.partial(on_device, mesh.shape["tm"], mesh.shape["space"]),
        mesh=mesh,
        in_specs=(
            P("tm", None, "space"),
            P("tm", None, "space"),
            P("space"),
            P(),
            P(),
            P(),
            P(),
            P(),
            P(None, "space"),
            P(None, "space"),
            P("space"),
        ),
        out_specs=(P("tm", None, "space"), P("tm", "space"), P()),
        check_vma=False,
    )
```

```python
import functools

import jax
import jax.numpy as jnp
from jax import lax
from jax.experimental import pallas as pl
from jax.experimental.pallas import tpu as pltpu
from jax.sharding import PartitionSpec as P

MESH = pl.DeviceIdType.MESH
F32 = jnp.float32
BF16 = jnp.bfloat16
D = 128
H = 64
FD = 32
R = 192
LAYERS = 8
NB = 128
E = 1024


def split(x):
    high = x.astype(BF16)
    return high, (x - high.astype(F32)).astype(BF16)


def dot(a, b):
    return jnp.dot(a, b, preferred_element_type=F32)


def iota(shape, dim):
    return lax.broadcasted_iota(jnp.int32, shape, dim)


def one_hot(mask):
    return jnp.where(mask, 1.0, 0.0).astype(BF16)


def column(row):
    eye = iota((NB, NB), 0) == iota((NB, NB), 1)
    return jnp.sum(jnp.where(eye, jnp.broadcast_to(row, (NB, NB)), 0), axis=1, keepdims=True)


def lookup(table, index):
    lane = jnp.broadcast_to(index & 127, (8, NB))
    line = jnp.broadcast_to(index >> 7, (8, NB))
    found = jnp.take_along_axis(table, lane, axis=1)
    return jnp.sum(jnp.where(line == iota((8, NB), 0), found, 0), axis=0, keepdims=True)


def layer(k):
    return slice(k * NB, (k + 1) * NB)


def rounds(n, known):
    out = []
    while known < n // 2:
        out.append(known)
        known *= 2
    return out


def near(n, radius):
    return [d for d in range(1, n) if min(d, n - d) <= radius]


TM_RADIUS, SPACE_RADIUS = 2, 1
OUT_PARTS = 2


def stack3(x):
    high, low = split(x)
    return jnp.concatenate([high, low, high], axis=0)


def over(x):
    return jnp.sum(x, axis=0, keepdims=True)


W = NB
SIDES = (slice(0, W), slice(E - W, E))
HALVES = (slice(W, 4 * W), slice(4 * W, E - W))
SIDE_LAYERS = (0, 7)
HALF_LAYERS = ((1, 2, 3), (4, 5, 6))


def part(q):
    return slice(q * 256, (q + 1) * 256)


def kernel(
    nt,
    ns,
    init_h,
    rhs_h,
    coef_h,
    stiff_h,
    binv_h,
    fproj_h,
    lift_h,
    tlift_h,
    nbr_h,
    bnd_h,
    send_h,
    init_v,
    dir_o,
    eta_o,
    tot_o,
    rhs_v,
    coef_v,
    weights_v,
    tables_v,
    send_v,
    place,
    start_v,
    xs,
    x3,
    t3,
    work,
    lat,
    jumps,
    pre,
    bpre,
    edge_out,
    edge_in,
    folded_v,
    resid,
    direc,
    rows,
    w_vol,
    w_lift,
    w_time,
    w_inv,
    w_both,
    w_rim,
    rim_out,
    rim_in,
    end_in,
    row_a,
    row_b,
    load_sem,
    end_send,
    end_recv,
    rim_send,
    rim_recv,
    sum_send,
    sum_recv,
    known_sem,
):
    t = lax.axis_index("tm")
    p = lax.axis_index("space")
    tm_rounds, space_rounds = rounds(nt, TM_RADIUS), rounds(ns, SPACE_RADIUS)
    tm_near, space_near = near(nt, TM_RADIUS), near(ns, SPACE_RADIUS)

    barrier = pltpu.get_barrier_semaphore()
    for axis, me, n, close in (("tm", t, nt, tm_near), ("space", p, ns, space_near)):
        for d in close:
            pl.semaphore_signal(barrier, inc=1, device_id={axis: lax.rem(me + d, n)}, device_id_type=MESH)

    def know(axis, k):
        me, n, reach, base = (t, nt, tm_rounds, 0) if axis == "tm" else (p, ns, space_rounds, len(tm_rounds))
        if 0 < k <= len(reach):
            pl.semaphore_wait(known_sem.at[base + k - 1], 2)
        if k < len(reach):
            for d in (reach[k], n - reach[k]):
                pl.semaphore_signal(known_sem.at[base + k], inc=1, device_id={axis: lax.rem(me + d, n)}, device_id_type=MESH)

    stiff_v = weights_v.at[pl.ds(0, D)]
    binv_v = weights_v.at[pl.ds(D, D)]
    fproj_v = weights_v.at[pl.ds(2 * D, R)]
    lift_v = weights_v.at[pl.ds(2 * D + R, R)]
    tlift_v = weights_v.at[pl.ds(2 * D + 2 * R, H)]
    nbr_v, bnd_v = tables_v.at[0], tables_v.at[1]
    for n, src, dst in (
        (0, send_h, send_v),
        (1, init_h.at[0], init_v),
        (2, fproj_h, fproj_v),
        (2, stiff_h, stiff_v),
        (2, lift_h, lift_v),
        (2, tlift_h, tlift_v),
        (2, binv_h, binv_v),
        (3, nbr_h, nbr_v),
        (3, bnd_h, bnd_v),
        (4, coef_h, coef_v),
        (5, rhs_h.at[0], rhs_v),
    ):
        pltpu.make_async_copy(src, dst, load_sem.at[n]).start()

    def arrived(ref, sem):
        pltpu.make_async_copy(ref, ref, sem).wait()

    arrived(send_v, load_sem.at[0])
    arrived(init_v, load_sem.at[1])
    arrived(weights_v, load_sem.at[2])
    arrived(tables_v, load_sem.at[3])
    arrived(coef_v, load_sem.at[4])
    up = {"tm": lax.rem(t + 1, nt)}
    upper_part = {"space": lax.rem(p + 1, ns)}
    lower_part = {"space": lax.rem(p + ns - 1, ns)}

    def send_end(k, n, src, columns):
        @pl.when(t < nt - 1)
        def _():
            pltpu.make_async_remote_copy(
                src_ref=src.at[pl.ds(H, H), columns],
                dst_ref=end_in.at[k, :, columns],
                send_sem=end_send.at[0],
                recv_sem=end_recv.at[n],
                device_id=up,
                device_id_type=MESH,
            ).start()

    def end_arrived(ref, n):
        @pl.when(t > 0)
        def _():
            arrived(ref, end_recv.at[n])

    def send_rims(k):
        for side, device, there in ((0, upper_part, p < ns - 1), (1, lower_part, p > 0)):

            @pl.when(there)
            def _():
                pltpu.make_async_remote_copy(
                    src_ref=rim_out.at[k, side],
                    dst_ref=rim_in.at[k, side],
                    send_sem=rim_send.at[side],
                    recv_sem=rim_recv.at[k, side],
                    device_id=device,
                    device_id_type=MESH,
                ).start()

    row, col = iota((R, R), 0), iota((R, R), 1)
    to_face = one_hot(col == (row & 31) * 6 + (row >> 5))
    lower = send_v[0:1, :] & (E - 1)
    upper = send_v[1:2, :] & (E - 1)
    column_ids = iota((E, NB), 0)
    ends = jnp.concatenate([one_hot(column_ids == lower), one_hot(column_ids == upper)], axis=1)
    both = dot(to_face, jnp.concatenate(split(fproj_v[...]), axis=1)).astype(BF16)
    fh, fl = both[:, :D], both[:, D:]
    w_vol[0:R, :] = jnp.concatenate([fh, fh, fl], axis=1)


    def table(ref, f):
        return jnp.concatenate([ref[f : f + 1, layer(k)] for k in range(8)], axis=0)

    first = p == 0
    chain_table = jnp.where(first, table(nbr_v, 0), table(nbr_v, 1)) & (E - 1)
    chain = [jnp.where(first, upper, lower)]
    for k in range(1, LAYERS):
        chain.append(lookup(chain_table, chain[-1]))
    slots = [jnp.where(first, chain[LAYERS - 1 - k], chain[k]) for k in range(LAYERS)]

    ih, il = split(init_v[...])
    xs[0:D, :] = ih
    xs[D : 2 * D, :] = il
    picked = dot(xs[0 : 2 * D, :], ends).astype(BF16)
    rim = dot(w_vol[0 : 2 * FD, :], jnp.concatenate([picked[:D], picked[D:], picked[:D]], axis=0))
    rim_out[0, 1] = rim[0:FD, 0:NB]
    rim_out[0, 0] = rim[FD : 2 * FD, NB : 2 * NB]

    for k in SIDE_LAYERS:
        place[:, layer(k)] = one_hot(column_ids == slots[k])
    for n, c in enumerate(SIDES):
        edge_out[n] = dot(xs[H:D, :], place[:, c]) + dot(xs[D + H : 2 * D, :], place[:, c])

    pl.semaphore_wait(barrier, len(tm_near) + len(space_near))

    @pl.when(t < nt - 1)
    def _():
        pltpu.make_async_remote_copy(
            src_ref=edge_out,
            dst_ref=edge_in,
            send_sem=end_send.at[1],
            recv_sem=end_recv.at[4],
            device_id=up,
            device_id_type=MESH,
        ).start()

    send_end(0, 0, init_v, pl.ds(0, E))
    send_rims(0)
    know("tm", 0)
    know("space", 0)

    base_col = column(slots[0])
    top_col = column(slots[LAYERS - 1])
    out_map = one_hot(top_col == upper)
    in_map = one_hot(column(upper) == slots[LAYERS - 1])
    lateral = []
    for f in range(2, 6):
        target = lookup(table(nbr_v, f) & (E - 1), slots[0])
        wall = lookup(table(bnd_v, f), slots[0])
        lateral.append(one_hot((base_col == target) & (wall == 0)))
    blank = jnp.zeros((NB, NB), BF16)
    lat_maps = [
        jnp.concatenate(
            [
                jnp.concatenate([lateral[2 * g], blank], axis=1),
                jnp.concatenate([blank, lateral[2 * g + 1]], axis=1),
            ],
            axis=0,
        )
        for g in range(2)
    ]

    sh, sl = split(stiff_v[...])
    w_vol[R : R + D, :] = jnp.concatenate([sh, sh, sl], axis=1)

    coef = coef_v[...]
    ch = coef.astype(BF16)
    rest = coef - ch.astype(F32)
    cm = rest.astype(BF16)
    cl = (rest - cm.astype(F32)).astype(BF16)
    xs[2 * D : 2 * D + 16, :] = jnp.concatenate([ch, cm, cl, jnp.zeros((13, E), BF16)], axis=0)
    for q in range(4):
        c = part(q)
        for k in {2 * q, 2 * q + 1} - set(SIDE_LAYERS):
            place[:, layer(k)] = one_hot(column_ids == slots[k])
        moved = dot(xs[...], place[:, c])
        coef_v[:, c] = moved[2 * D : 2 * D + 1] + moved[2 * D + 1 : 2 * D + 2] + moved[2 * D + 2 : 2 * D + 3]
        xh = moved[0:D].astype(BF16)
        x3[0:D, c] = xh
        x3[D : 2 * D, c] = moved[D : 2 * D].astype(BF16)
        x3[2 * D : 3 * D, c] = xh
        start_v[:, c] = moved[0:H] + moved[D : D + H]
    coef = coef_v[...]
    inverse_coef = 1.0 / coef

    def wide(high, low):
        return jnp.concatenate([high, high, low], axis=0).astype(F32).T.astype(BF16)

    both = dot(to_face, jnp.concatenate(split(lift_v[...]), axis=1))
    w_lift[...] = wide(both[:, :D], both[:, D:])
    lift_high, lift_low = both[:, :D].astype(BF16), both[:, D:].astype(BF16)
    th, tl = split(tlift_v[...])
    w_time[...] = wide(th, tl)
    bh, bl = split(binv_v[...])
    w_inv[...] = jnp.concatenate([bh, bh, bl], axis=1)
    both = lax.dot_general(
        jnp.concatenate([th, tl, th], axis=1), w_inv[...], (((1,), (1,)), ((), ())), preferred_element_type=F32
    )
    w_both[...] = wide(*split(both))
    for f in range(2):
        high, low = lift_high[f * FD : (f + 1) * FD], lift_low[f * FD : (f + 1) * FD]
        both = lax.dot_general(
            jnp.concatenate([high, low, high], axis=1), w_inv[...], (((1,), (1,)), ((), ())), preferred_element_type=F32
        )
        w_rim[f, 0:D, :] = wide(high, low)
        w_rim[f, D : 2 * D, :] = wide(*split(both))

    def lateral_jumps(k, layers):
        count = len(layers) * 2 * FD
        for g in range(2):
            a, b = 2 + 2 * g, 3 + 2 * g
            for n, x in enumerate(layers):
                for side, f in ((0, b), (1, a)):
                    high, low = split(work[f * FD : (f + 1) * FD, layer(x)])
                    lat[n * 2 * FD : n * 2 * FD + FD, layer(side)] = high
                    lat[n * 2 * FD + FD : (n + 1) * 2 * FD, layer(side)] = low
            seen = dot(lat[0:count], lat_maps[g])
            for n, x in enumerate(layers):
                both = seen[n * 2 * FD : n * 2 * FD + FD] + seen[n * 2 * FD + FD : (n + 1) * 2 * FD]
                for side, f in ((0, a), (1, b)):
                    jumps[k, f * FD : (f + 1) * FD, layer(x)] = work[f * FD : (f + 1) * FD, layer(x)] - both[:, layer(side)]
        for x in layers:
            if x > 0:
                jumps[k, 0:FD, layer(x)] = work[0:FD, layer(x)] - work[FD : 2 * FD, layer(x - 1)]
            if x < LAYERS - 1:
                jumps[k, FD : 2 * FD, layer(x)] = work[FD : 2 * FD, layer(x)] - work[0:FD, layer(x + 1)]

    rim_blocks = ((0, layer(0)), (1, layer(LAYERS - 1)))

    def without_rims(k):
        for f, c in rim_blocks:
            jumps[k, f * FD : (f + 1) * FD, c] = jnp.zeros((FD, NB), F32)

    def rims_arrived(k):
        for side, there in ((0, p > 0), (1, p < ns - 1)):

            @pl.when(there)
            def _():
                arrived(rim_in.at[k, side], rim_recv.at[k, side])

    def rim_terms(k):
        turned = dot(jnp.concatenate(split(rim_in[k, 1]), axis=0), in_map)
        outside = (
            jnp.where(p == 0, 0.0, rim_in[k, 0]),
            jnp.where(p == ns - 1, 0.0, turned[:FD] + turned[FD:]),
        )
        found = []
        for f, c in rim_blocks:
            block = work[f * FD : (f + 1) * FD, c] - outside[f]
            jumps[k, f * FD : (f + 1) * FD, c] = block
            added = dot(w_rim[f, 0 : D if k else 2 * D, :], stack3(block))
            found.append((f, c, block, added))
        return found

    def apply_local(k, c):
        return coef[:, c] * work[R : R + D, c] + dot(w_lift[...], stack3(jumps[k, 0:R, c]))

    def move_rhs(c):
        moved = dot(xs[0 : 2 * D, :], place[:, c])
        pre[:, c] = moved[:D] + moved[D:]

    def start_residual(c):
        local = pre[:, c] - apply_local(0, c)
        pre[:, c] = local
        bpre[:, c] = dot(w_inv[...], stack3(local)) * inverse_coef[:, c]

    arrived(rhs_v, load_sem.at[5])
    work[...] = dot(w_vol[...], x3[...])
    rh, rl = split(rhs_v[...])
    xs[0:D, :] = rh
    xs[D : 2 * D, :] = rl
    lateral_jumps(0, SIDE_LAYERS)
    for c in SIDES:
        move_rhs(c)
    without_rims(0)
    for c in SIDES:
        start_residual(c)

    know("tm", 1)
    know("space", 1)
    end_arrived(edge_in, 4)

    def slab_start(c, before):
        jump = start_v[:, c] - jnp.where(t == 0, 0.0, before)
        jumps[0, R:, c] = jump
        t3[:, c] = stack3(jump)
        direc[:, c] = bpre[:, c] - dot(w_both[...], t3[:, c]) * inverse_coef[:, c]

    for n, c in enumerate(SIDES):
        slab_start(c, edge_in[n])
    rims_arrived(0)
    for _, c, _, added in rim_terms(0):
        pre[:, c] = pre[:, c] - added[:D]
        direc[:, c] = direc[:, c] - added[D:] * inverse_coef[:, c]
    for c in SIDES:
        x3[:, c] = stack3(direc[:, c])
    for n, c in enumerate(SIDES):
        send_end(1, 1 + n, direc, pl.ds(c.start, W))
    rim_out[1, 1] = dot(w_vol[0:FD, :], x3[:, layer(0)])
    rim = dot(w_vol[FD : 2 * FD, :], x3[:, layer(LAYERS - 1)])
    turned = dot(jnp.concatenate(split(rim), axis=0), out_map)
    rim_out[1, 0] = turned[:FD] + turned[FD:]
    send_rims(1)
    for n, c in enumerate(HALVES):
        lateral_jumps(0, HALF_LAYERS[n])
        move_rhs(c)
        start_residual(c)
        if n == 0:
            end_arrived(end_in.at[0], 0)
        moved = dot(jnp.concatenate(split(end_in[0]), axis=0), place[:, c])
        slab_start(c, moved[:H] + moved[H:])
        send_end(1, 3 + 2 * n, direc, pl.ds(c.start, c.stop - c.start))
        x3[:, c] = stack3(direc[:, c])
    know("space", 2)

    work[...] = dot(w_vol[...], x3[...])
    residual = pre[...] - dot(w_time[...], t3[...])
    resid[...] = residual
    lateral_jumps(1, range(LAYERS))
    without_rims(1)
    pre[...] = apply_local(1, slice(0, E))
    j0, j1 = jumps[0, :R], jumps[1, :R]
    rows[2:3, :] = over(residual * residual) + 0.5 * over(j0 * j0) + over(jumps[0, R:] * jumps[0, R:])
    rows[3:4, :] = over(j0 * j1)
    rows[4:5, :] = 0.5 * over(j1 * j1)
    def image_sums(c):
        jump = direc[0:H, c] - jnp.where(t == 0, 0.0, end_in[1, :, c])
        image = pre[:, c] + dot(w_time[...], stack3(jump))
        cross = over(resid[:, c] * image)
        square = over(image * image)
        found = jnp.concatenate(
            [
                cross,
                square,
                rows[2:3, c],
                rows[3:4, c] + 2.0 * over(jumps[0, R:, c] * jump) - 2.0 * cross,
                rows[4:5, c] + square + over(jump * jump),
                jnp.zeros((3, c.stop - c.start), F32),
            ],
            axis=0,
        )
        rows[:, c] = found
        return sum(found[:, layer(k)] for k in range((c.stop - c.start) // NB))

    def middle_sums():
        for n, c in enumerate(HALVES):
            end_arrived(end_in.at[1, :, pl.ds(c.start, c.stop - c.start)], 3 + 2 * n)
            found = image_sums(c)
            folded_v[...] = folded_v[...] + found if n else found

    rims_last = lax.rem(p, LAYERS) == 0

    @pl.when(rims_last)
    def _():
        middle_sums()

    for n, c in enumerate(SIDES):
        end_arrived(end_in.at[1, :, pl.ds(c.start, W)], 1 + n)
    rims_arrived(1)
    for f, c, block, added in rim_terms(1):
        pre[:, c] = pre[:, c] + added
        rows[3:4, c] = rows[3:4, c] + over(jumps[0, f * FD : (f + 1) * FD, c] * block)
        rows[4:5, c] = rows[4:5, c] + 0.5 * over(block * block)

    folded = image_sums(SIDES[0]) + image_sums(SIDES[1])

    @pl.when(jnp.logical_not(rims_last))
    def _():
        middle_sums()

    folded = folded + folded_v[...]
    sums = jnp.sum(folded, axis=1, keepdims=True)
    diagonal = iota((8, NB), 0) == iota((8, NB), 1)
    message = jnp.sum(jnp.where(diagonal, sums, 0.0), axis=0, keepdims=True)

    def exchange(buf, me, count, axis, n):
        for d in range(1, count):
            pltpu.make_async_remote_copy(
                src_ref=buf.at[me],
                dst_ref=buf.at[me],
                send_sem=sum_send.at[0],
                recv_sem=sum_recv.at[n],
                device_id={axis: lax.rem(me + d, count)},
                device_id_type=MESH,
            ).start()
        others = buf.at[pl.ds(0, count - 1)]
        return pltpu.make_async_copy(others, others, sum_recv.at[n])

    know("tm", 2)
    row_a[t] = message
    got = exchange(row_a, t, nt, "tm", 0)
    eh = rows[...].astype(BF16)
    rest = rows[...] - eh.astype(F32)
    em = rest.astype(BF16)
    el = (rest - em.astype(F32)).astype(BF16)
    back = lax.dot_general(
        jnp.concatenate([x3[0 : 2 * D, :], eh, em, el, jnp.zeros((8, E), BF16)], axis=0),
        place[...],
        (((1,), (1,)), ((), ())),
        preferred_element_type=F32,
    )
    dir_o[...] = back[:D] + back[D : 2 * D]
    eta_o[...] = back[2 * D : 2 * D + 8] + back[2 * D + 8 : 2 * D + 16] + back[2 * D + 16 : 2 * D + 24]
    know("space", 3)
    got.wait()
    total = row_a[0]
    for d in range(1, nt):
        total = total + row_a[d]
    know("space", 4)
    row_b[p] = total
    exchange(row_b, p, ns, "space", 1).wait()
    total = row_b[0]
    for d in range(1, ns):
        total = total + row_b[d]
    tot_o[...] = total

    @pl.when(t < nt - 1)
    def _():
        arrived(end_in, end_send.at[0])
        arrived(edge_in, end_send.at[1])

    for side, there in ((0, p < ns - 1), (1, p > 0)):

        @pl.when(there)
        def _():
            arrived(rim_in.at[:, side], rim_send.at[side])

    arrived(row_b.at[pl.ds(0, nt + ns - 2)], sum_send.at[0])


def finish(count, init_v, dir_v, eta_v, tot_v, out_h, ind_h, est_h, out_v, ind_v, est_v, sem):
    cross, square, base, mixed, quad = (tot_v[0:1, k : k + 1] for k in range(5))
    step = cross / square
    copies = []

    def send(src, dst):
        copies.append(pltpu.make_async_copy(src, dst, sem.at[len(copies)]))
        copies[-1].start()

    for k in range(OUT_PARTS):
        part_rows = pl.ds(k * (D // OUT_PARTS), D // OUT_PARTS)
        out_v[part_rows] = init_v[part_rows] + step * dir_v[part_rows]
        send(out_v.at[part_rows], out_h.at[0, part_rows])
    eta_total = base + step * mixed + step * step * quad
    eta = eta_v[2:3] + step * eta_v[3:4] + step * step * eta_v[4:5]
    ind_v[...] = eta * count / eta_total
    send(ind_v, ind_h)
    est_v[...] = jnp.broadcast_to(jnp.sqrt(eta_total / count), (1, NB))
    send(est_v, est_h)
    for copy in copies:
        copy.wait()


def on_device(nt, ns, initial, rhs, coef, stiffness, block_inverse, face_proj, lift, time_lift, neighbour, boundary, send_list):
    vmem = pltpu.VMEM
    hbm_spec = pl.BlockSpec(memory_space=pltpu.HBM)
    vmem_spec = pl.BlockSpec(memory_space=vmem)
    dma = pltpu.SemaphoreType.DMA
    iterate, direction, eta, totals = pl.pallas_call(
        functools.partial(kernel, nt, ns),
        out_shape=(
            jax.ShapeDtypeStruct((D, E), F32),
            jax.ShapeDtypeStruct((D, E), F32),
            jax.ShapeDtypeStruct((8, E), F32),
            jax.ShapeDtypeStruct((1, NB), F32),
        ),
        in_specs=[hbm_spec] * 11,
        out_specs=[vmem_spec] * 4,
        scratch_shapes=[
            vmem((D, E), F32),
            vmem((1, E), F32),
            vmem((2 * D + 2 * R + H, D), F32),
            vmem((2, 6, E), jnp.int32),
            vmem((2, NB), jnp.int32),
            vmem((E, E), BF16),
            vmem((H, E), F32),
            vmem((2 * D + 16, E), BF16),
            vmem((3 * D, E), BF16),
            vmem((3 * H, E), BF16),
            vmem((R + D, E), F32),
            vmem((LAYERS * 2 * FD, 2 * NB), BF16),
            vmem((2, 256, E), F32),
            vmem((D, E), F32),
            vmem((D, E), F32),
            vmem((2, H, NB), F32),
            vmem((2, H, NB), F32),
            vmem((8, NB), F32),
            vmem((D, E), F32),
            vmem((D, E), F32),
            vmem((8, E), F32),
            vmem((R + D, 3 * D), BF16),
            vmem((D, 3 * R), BF16),
            vmem((D, 3 * H), BF16),
            vmem((D, 3 * D), BF16),
            vmem((D, 3 * H), BF16),
            vmem((2, 2 * D, 3 * FD), BF16),
            vmem((2, 2, FD, NB), F32),
            vmem((2, 2, FD, NB), F32),
            vmem((2, H, E), F32),
            vmem((nt, 1, NB), F32),
            vmem((nt + ns, 1, NB), F32),
            dma((6,)),
            dma((2,)),
            dma((6,)),
            dma((2,)),
            dma((2, 2)),
            dma((1,)),
            dma((2,)),
            pltpu.SemaphoreType.REGULAR((max(1, len(rounds(nt, TM_RADIUS)) + len(rounds(ns, SPACE_RADIUS))),)),
        ],
        compiler_params=pltpu.CompilerParams(collective_id=0, has_side_effects=True, vmem_limit_bytes=40 * 1024 * 1024),
        cost_estimate=pl.CostEstimate(flops=4 * 10**9, bytes_accessed=3 * 2**20, transcendentals=0),
    )(
        *(
            pltpu.with_memory_space_constraint(x, pltpu.HBM)
            for x in (
                initial,
                rhs,
                coef.reshape(1, E),
                stiffness,
                block_inverse,
                face_proj,
                lift.T,
                time_lift.T,
                neighbour,
                boundary,
                send_list.reshape(2, NB),
            )
        )
    )
    smoothed, indicator, estimate = pl.pallas_call(
        functools.partial(finish, float(E * nt * ns)),
        out_shape=(
            jax.ShapeDtypeStruct((1, D, E), F32),
            jax.ShapeDtypeStruct((1, E), F32),
            jax.ShapeDtypeStruct((1, NB), F32),
        ),
        in_specs=[vmem_spec] * 4,
        out_specs=[hbm_spec] * 3,
        scratch_shapes=[
            vmem((D, E), F32),
            vmem((1, E), F32),
            vmem((1, NB), F32),
            dma((OUT_PARTS + 2,)),
        ],
        compiler_params=pltpu.CompilerParams(vmem_limit_bytes=8 * 1024 * 1024),
        cost_estimate=pl.CostEstimate(flops=3 * 10**5, bytes_accessed=2**20, transcendentals=0),
    )(iterate, direction, eta, totals)
    return smoothed, indicator, estimate[0, :1]


def solution(mesh):
    return jax.shard_map(
        functools.partial(on_device, mesh.shape["tm"], mesh.shape["space"]),
        mesh=mesh,
        in_specs=(
            P("tm", None, "space"),
            P("tm", None, "space"),
            P("space"),
            P(),
            P(),
            P(),
            P(),
            P(),
            P(None, "space"),
            P(None, "space"),
            P("space"),
        ),
        out_specs=(P("tm", None, "space"), P("tm", "space"), P()),
        check_vma=False,
    )
```

```python
import functools

import jax
import jax.numpy as jnp
from jax import lax
from jax.experimental import pallas as pl
from jax.experimental.pallas import tpu as pltpu
from jax.sharding import PartitionSpec as P

MESH = pl.DeviceIdType.MESH
F32 = jnp.float32
BF16 = jnp.bfloat16
D = 128
H = 64
FD = 32
R = 192
LAYERS = 8
NB = 128
E = 1024


def split(x):
    high = x.astype(BF16)
    return high, (x - high.astype(F32)).astype(BF16)


def dot(a, b):
    return jnp.dot(a, b, preferred_element_type=F32)


def iota(shape, dim):
    return lax.broadcasted_iota(jnp.int32, shape, dim)


def one_hot(mask):
    return jnp.where(mask, 1.0, 0.0).astype(BF16)


def column(row):
    eye = iota((NB, NB), 0) == iota((NB, NB), 1)
    return jnp.sum(jnp.where(eye, jnp.broadcast_to(row, (NB, NB)), 0), axis=1, keepdims=True)


def lookup(table, index):
    lane = jnp.broadcast_to(index & 127, (8, NB))
    line = jnp.broadcast_to(index >> 7, (8, NB))
    found = jnp.take_along_axis(table, lane, axis=1)
    return jnp.sum(jnp.where(line == iota((8, NB), 0), found, 0), axis=0, keepdims=True)


def layer(k):
    return slice(k * NB, (k + 1) * NB)


def rounds(n, known):
    out = []
    while known < n // 2:
        out.append(known)
        known *= 2
    return out


def near(n, radius):
    return [d for d in range(1, n) if min(d, n - d) <= radius]


TM_RADIUS, SPACE_RADIUS = 2, 1
OUT_PARTS = 2


def stack3(x):
    high, low = split(x)
    return jnp.concatenate([high, low, high], axis=0)


def over(x):
    return jnp.sum(x, axis=0, keepdims=True)


W = NB
SIDES = (slice(0, W), slice(E - W, E))
HALVES = (slice(W, 4 * W), slice(4 * W, E - W))
SIDE_LAYERS = (0, 7)
HALF_LAYERS = ((1, 2, 3), (4, 5, 6))


def part(q):
    return slice(q * 256, (q + 1) * 256)


def kernel(
    nt,
    ns,
    init_h,
    rhs_h,
    coef_h,
    stiff_h,
    binv_h,
    fproj_h,
    lift_h,
    tlift_h,
    nbr_h,
    bnd_h,
    send_h,
    init_v,
    dir_o,
    eta_o,
    tot_o,
    rhs_v,
    coef_v,
    weights_v,
    tables_v,
    send_v,
    place,
    start_v,
    xs,
    x3,
    t3,
    work,
    lat,
    jumps,
    pre,
    bpre,
    edge_out,
    edge_in,
    resid,
    direc,
    rows,
    w_vol,
    w_lift,
    w_time,
    w_inv,
    w_both,
    w_rim,
    rim_out,
    rim_in,
    end_in,
    row_a,
    row_b,
    load_sem,
    end_send,
    end_recv,
    rim_send,
    rim_recv,
    sum_send,
    sum_recv,
    known_sem,
):
    t = lax.axis_index("tm")
    p = lax.axis_index("space")
    tm_rounds, space_rounds = rounds(nt, TM_RADIUS), rounds(ns, SPACE_RADIUS)
    tm_near, space_near = near(nt, TM_RADIUS), near(ns, SPACE_RADIUS)

    barrier = pltpu.get_barrier_semaphore()
    for axis, me, n, close in (("tm", t, nt, tm_near), ("space", p, ns, space_near)):
        for d in close:
            pl.semaphore_signal(barrier, inc=1, device_id={axis: lax.rem(me + d, n)}, device_id_type=MESH)

    def know(axis, k):
        me, n, reach, base = (t, nt, tm_rounds, 0) if axis == "tm" else (p, ns, space_rounds, len(tm_rounds))
        if 0 < k <= len(reach):
            pl.semaphore_wait(known_sem.at[base + k - 1], 2)
        if k < len(reach):
            for d in (reach[k], n - reach[k]):
                pl.semaphore_signal(known_sem.at[base + k], inc=1, device_id={axis: lax.rem(me + d, n)}, device_id_type=MESH)

    stiff_v = weights_v.at[pl.ds(0, D)]
    binv_v = weights_v.at[pl.ds(D, D)]
    fproj_v = weights_v.at[pl.ds(2 * D, R)]
    lift_v = weights_v.at[pl.ds(2 * D + R, R)]
    tlift_v = weights_v.at[pl.ds(2 * D + 2 * R, H)]
    nbr_v, bnd_v = tables_v.at[0], tables_v.at[1]
    for n, src, dst in (
        (0, send_h, send_v),
        (1, init_h.at[0], init_v),
        (2, fproj_h, fproj_v),
        (2, stiff_h, stiff_v),
        (2, lift_h, lift_v),
        (2, tlift_h, tlift_v),
        (2, binv_h, binv_v),
        (3, nbr_h, nbr_v),
        (3, bnd_h, bnd_v),
        (4, coef_h, coef_v),
        (5, rhs_h.at[0], rhs_v),
    ):
        pltpu.make_async_copy(src, dst, load_sem.at[n]).start()

    def arrived(ref, sem):
        pltpu.make_async_copy(ref, ref, sem).wait()

    arrived(send_v, load_sem.at[0])
    arrived(init_v, load_sem.at[1])
    arrived(weights_v, load_sem.at[2])
    arrived(tables_v, load_sem.at[3])
    arrived(coef_v, load_sem.at[4])
    up = {"tm": lax.rem(t + 1, nt)}
    upper_part = {"space": lax.rem(p + 1, ns)}
    lower_part = {"space": lax.rem(p + ns - 1, ns)}

    def send_end(k, n, src, columns):
        @pl.when(t < nt - 1)
        def _():
            pltpu.make_async_remote_copy(
                src_ref=src.at[pl.ds(H, H), columns],
                dst_ref=end_in.at[k, :, columns],
                send_sem=end_send.at[0],
                recv_sem=end_recv.at[n],
                device_id=up,
                device_id_type=MESH,
            ).start()

    def end_arrived(ref, n):
        @pl.when(t > 0)
        def _():
            arrived(ref, end_recv.at[n])

    def send_rims(k):
        for side, device, there in ((0, upper_part, p < ns - 1), (1, lower_part, p > 0)):

            @pl.when(there)
            def _():
                pltpu.make_async_remote_copy(
                    src_ref=rim_out.at[k, side],
                    dst_ref=rim_in.at[k, side],
                    send_sem=rim_send.at[side],
                    recv_sem=rim_recv.at[k, side],
                    device_id=device,
                    device_id_type=MESH,
                ).start()

    row, col = iota((R, R), 0), iota((R, R), 1)
    to_face = one_hot(col == (row & 31) * 6 + (row >> 5))
    lower = send_v[0:1, :] & (E - 1)
    upper = send_v[1:2, :] & (E - 1)
    column_ids = iota((E, NB), 0)
    ends = jnp.concatenate([one_hot(column_ids == lower), one_hot(column_ids == upper)], axis=1)
    both = dot(to_face, jnp.concatenate(split(fproj_v[...]), axis=1)).astype(BF16)
    fh, fl = both[:, :D], both[:, D:]
    w_vol[0:R, :] = jnp.concatenate([fh, fh, fl], axis=1)


    def table(ref, f):
        return jnp.concatenate([ref[f : f + 1, layer(k)] for k in range(8)], axis=0)

    first = p == 0
    chain_table = jnp.where(first, table(nbr_v, 0), table(nbr_v, 1)) & (E - 1)
    chain = [jnp.where(first, upper, lower)]
    for k in range(1, LAYERS):
        chain.append(lookup(chain_table, chain[-1]))
    slots = [jnp.where(first, chain[LAYERS - 1 - k], chain[k]) for k in range(LAYERS)]

    ih, il = split(init_v[...])
    xs[0:D, :] = ih
    xs[D : 2 * D, :] = il
    picked = dot(xs[0 : 2 * D, :], ends).astype(BF16)
    rim = dot(w_vol[0 : 2 * FD, :], jnp.concatenate([picked[:D], picked[D:], picked[:D]], axis=0))
    rim_out[0, 1] = rim[0:FD, 0:NB]
    rim_out[0, 0] = rim[FD : 2 * FD, NB : 2 * NB]

    for k in SIDE_LAYERS:
        place[:, layer(k)] = one_hot(column_ids == slots[k])
    for n, c in enumerate(SIDES):
        edge_out[n] = dot(xs[H:D, :], place[:, c]) + dot(xs[D + H : 2 * D, :], place[:, c])

    pl.semaphore_wait(barrier, len(tm_near) + len(space_near))

    @pl.when(t < nt - 1)
    def _():
        pltpu.make_async_remote_copy(
            src_ref=edge_out,
            dst_ref=edge_in,
            send_sem=end_send.at[1],
            recv_sem=end_recv.at[4],
            device_id=up,
            device_id_type=MESH,
        ).start()

    send_end(0, 0, init_v, pl.ds(0, E))
    send_rims(0)
    know("tm", 0)
    know("space", 0)

    base_col = column(slots[0])
    top_col = column(slots[LAYERS - 1])
    out_map = one_hot(top_col == upper)
    in_map = one_hot(column(upper) == slots[LAYERS - 1])
    lateral = []
    for f in range(2, 6):
        target = lookup(table(nbr_v, f) & (E - 1), slots[0])
        wall = lookup(table(bnd_v, f), slots[0])
        lateral.append(one_hot((base_col == target) & (wall == 0)))
    blank = jnp.zeros((NB, NB), BF16)
    lat_maps = [
        jnp.concatenate(
            [
                jnp.concatenate([lateral[2 * g], blank], axis=1),
                jnp.concatenate([blank, lateral[2 * g + 1]], axis=1),
            ],
            axis=0,
        )
        for g in range(2)
    ]

    sh, sl = split(stiff_v[...])
    w_vol[R : R + D, :] = jnp.concatenate([sh, sh, sl], axis=1)

    coef = coef_v[...]
    ch = coef.astype(BF16)
    rest = coef - ch.astype(F32)
    cm = rest.astype(BF16)
    cl = (rest - cm.astype(F32)).astype(BF16)
    xs[2 * D : 2 * D + 16, :] = jnp.concatenate([ch, cm, cl, jnp.zeros((13, E), BF16)], axis=0)
    for q in range(4):
        c = part(q)
        for k in {2 * q, 2 * q + 1} - set(SIDE_LAYERS):
            place[:, layer(k)] = one_hot(column_ids == slots[k])
        moved = dot(xs[...], place[:, c])
        coef_v[:, c] = moved[2 * D : 2 * D + 1] + moved[2 * D + 1 : 2 * D + 2] + moved[2 * D + 2 : 2 * D + 3]
        xh = moved[0:D].astype(BF16)
        x3[0:D, c] = xh
        x3[D : 2 * D, c] = moved[D : 2 * D].astype(BF16)
        x3[2 * D : 3 * D, c] = xh
        start_v[:, c] = moved[0:H] + moved[D : D + H]
    coef = coef_v[...]
    inverse_coef = 1.0 / coef

    def wide(high, low):
        return jnp.concatenate([high, high, low], axis=0).astype(F32).T.astype(BF16)

    both = dot(to_face, jnp.concatenate(split(lift_v[...]), axis=1))
    w_lift[...] = wide(both[:, :D], both[:, D:])
    lift_high, lift_low = both[:, :D].astype(BF16), both[:, D:].astype(BF16)
    th, tl = split(tlift_v[...])
    w_time[...] = wide(th, tl)
    bh, bl = split(binv_v[...])
    w_inv[...] = jnp.concatenate([bh, bh, bl], axis=1)
    both = lax.dot_general(
        jnp.concatenate([th, tl, th], axis=1), w_inv[...], (((1,), (1,)), ((), ())), preferred_element_type=F32
    )
    w_both[...] = wide(*split(both))
    for f in range(2):
        high, low = lift_high[f * FD : (f + 1) * FD], lift_low[f * FD : (f + 1) * FD]
        both = lax.dot_general(
            jnp.concatenate([high, low, high], axis=1), w_inv[...], (((1,), (1,)), ((), ())), preferred_element_type=F32
        )
        w_rim[f, 0:D, :] = wide(high, low)
        w_rim[f, D : 2 * D, :] = wide(*split(both))

    def lateral_jumps(k, layers):
        count = len(layers) * 2 * FD
        for g in range(2):
            a, b = 2 + 2 * g, 3 + 2 * g
            for n, x in enumerate(layers):
                for side, f in ((0, b), (1, a)):
                    high, low = split(work[f * FD : (f + 1) * FD, layer(x)])
                    lat[n * 2 * FD : n * 2 * FD + FD, layer(side)] = high
                    lat[n * 2 * FD + FD : (n + 1) * 2 * FD, layer(side)] = low
            seen = dot(lat[0:count], lat_maps[g])
            for n, x in enumerate(layers):
                both = seen[n * 2 * FD : n * 2 * FD + FD] + seen[n * 2 * FD + FD : (n + 1) * 2 * FD]
                for side, f in ((0, a), (1, b)):
                    jumps[k, f * FD : (f + 1) * FD, layer(x)] = work[f * FD : (f + 1) * FD, layer(x)] - both[:, layer(side)]
        for x in layers:
            if x > 0:
                jumps[k, 0:FD, layer(x)] = work[0:FD, layer(x)] - work[FD : 2 * FD, layer(x - 1)]
            if x < LAYERS - 1:
                jumps[k, FD : 2 * FD, layer(x)] = work[FD : 2 * FD, layer(x)] - work[0:FD, layer(x + 1)]

    rim_blocks = ((0, layer(0)), (1, layer(LAYERS - 1)))

    def without_rims(k):
        for f, c in rim_blocks:
            jumps[k, f * FD : (f + 1) * FD, c] = jnp.zeros((FD, NB), F32)

    def rims_arrived(k):
        for side, there in ((0, p > 0), (1, p < ns - 1)):

            @pl.when(there)
            def _():
                arrived(rim_in.at[k, side], rim_recv.at[k, side])

    def rim_terms(k):
        turned = dot(jnp.concatenate(split(rim_in[k, 1]), axis=0), in_map)
        outside = (
            jnp.where(p == 0, 0.0, rim_in[k, 0]),
            jnp.where(p == ns - 1, 0.0, turned[:FD] + turned[FD:]),
        )
        found = []
        for f, c in rim_blocks:
            block = work[f * FD : (f + 1) * FD, c] - outside[f]
            jumps[k, f * FD : (f + 1) * FD, c] = block
            added = dot(w_rim[f, 0 : D if k else 2 * D, :], stack3(block))
            found.append((f, c, block, added))
        return found

    def apply_local(k, c):
        return coef[:, c] * work[R : R + D, c] + dot(w_lift[...], stack3(jumps[k, 0:R, c]))

    def move_rhs(c):
        moved = dot(xs[0 : 2 * D, :], place[:, c])
        pre[:, c] = moved[:D] + moved[D:]

    def start_residual(c):
        local = pre[:, c] - apply_local(0, c)
        pre[:, c] = local
        bpre[:, c] = dot(w_inv[...], stack3(local)) * inverse_coef[:, c]

    arrived(rhs_v, load_sem.at[5])
    work[...] = dot(w_vol[...], x3[...])
    rh, rl = split(rhs_v[...])
    xs[0:D, :] = rh
    xs[D : 2 * D, :] = rl
    lateral_jumps(0, SIDE_LAYERS)
    for c in SIDES:
        move_rhs(c)
    without_rims(0)
    for c in SIDES:
        start_residual(c)

    know("tm", 1)
    know("space", 1)
    end_arrived(edge_in, 4)

    def slab_start(c, before):
        jump = start_v[:, c] - jnp.where(t == 0, 0.0, before)
        jumps[0, R:, c] = jump
        t3[:, c] = stack3(jump)
        direc[:, c] = bpre[:, c] - dot(w_both[...], t3[:, c]) * inverse_coef[:, c]

    for n, c in enumerate(SIDES):
        slab_start(c, edge_in[n])
    rims_arrived(0)
    for _, c, _, added in rim_terms(0):
        pre[:, c] = pre[:, c] - added[:D]
        direc[:, c] = direc[:, c] - added[D:] * inverse_coef[:, c]
    for c in SIDES:
        x3[:, c] = stack3(direc[:, c])
    for n, c in enumerate(SIDES):
        send_end(1, 1 + n, direc, pl.ds(c.start, W))
    rim_out[1, 1] = dot(w_vol[0:FD, :], x3[:, layer(0)])
    rim = dot(w_vol[FD : 2 * FD, :], x3[:, layer(LAYERS - 1)])
    turned = dot(jnp.concatenate(split(rim), axis=0), out_map)
    rim_out[1, 0] = turned[:FD] + turned[FD:]
    send_rims(1)
    for n, c in enumerate(HALVES):
        lateral_jumps(0, HALF_LAYERS[n])
        move_rhs(c)
        start_residual(c)
        if n == 0:
            end_arrived(end_in.at[0], 0)
        moved = dot(jnp.concatenate(split(end_in[0]), axis=0), place[:, c])
        slab_start(c, moved[:H] + moved[H:])
        send_end(1, 3 + 2 * n, direc, pl.ds(c.start, c.stop - c.start))
        x3[:, c] = stack3(direc[:, c])
    know("space", 2)

    work[...] = dot(w_vol[...], x3[...])
    residual = pre[...] - dot(w_time[...], t3[...])
    resid[...] = residual
    lateral_jumps(1, range(LAYERS))
    without_rims(1)
    pre[...] = apply_local(1, slice(0, E))
    j0, j1 = jumps[0, :R], jumps[1, :R]
    rows[2:3, :] = over(residual * residual) + 0.5 * over(j0 * j0) + over(jumps[0, R:] * jumps[0, R:])
    rows[3:4, :] = over(j0 * j1)
    rows[4:5, :] = 0.5 * over(j1 * j1)
    def image_sums(c):
        jump = direc[0:H, c] - jnp.where(t == 0, 0.0, end_in[1, :, c])
        image = pre[:, c] + dot(w_time[...], stack3(jump))
        cross = over(resid[:, c] * image)
        square = over(image * image)
        found = jnp.concatenate(
            [
                cross,
                square,
                rows[2:3, c],
                rows[3:4, c] + 2.0 * over(jumps[0, R:, c] * jump) - 2.0 * cross,
                rows[4:5, c] + square + over(jump * jump),
                jnp.zeros((3, c.stop - c.start), F32),
            ],
            axis=0,
        )
        rows[:, c] = found
        return sum(found[:, layer(k)] for k in range((c.stop - c.start) // NB))

    for n, c in enumerate(SIDES):
        end_arrived(end_in.at[1, :, pl.ds(c.start, W)], 1 + n)
    rims_arrived(1)
    for f, c, block, added in rim_terms(1):
        pre[:, c] = pre[:, c] + added
        rows[3:4, c] = rows[3:4, c] + over(jumps[0, f * FD : (f + 1) * FD, c] * block)
        rows[4:5, c] = rows[4:5, c] + 0.5 * over(block * block)

    folded = image_sums(SIDES[0]) + image_sums(SIDES[1])

    for n, c in enumerate(HALVES):
        end_arrived(end_in.at[1, :, pl.ds(c.start, c.stop - c.start)], 3 + 2 * n)
        folded = folded + image_sums(c)
    sums = jnp.sum(folded, axis=1, keepdims=True)
    diagonal = iota((8, NB), 0) == iota((8, NB), 1)
    message = jnp.sum(jnp.where(diagonal, sums, 0.0), axis=0, keepdims=True)

    def exchange(buf, me, count, axis, n):
        for d in range(1, count):
            pltpu.make_async_remote_copy(
                src_ref=buf.at[me],
                dst_ref=buf.at[me],
                send_sem=sum_send.at[0],
                recv_sem=sum_recv.at[n],
                device_id={axis: lax.rem(me + d, count)},
                device_id_type=MESH,
            ).start()
        others = buf.at[pl.ds(0, count - 1)]
        return pltpu.make_async_copy(others, others, sum_recv.at[n])

    know("tm", 2)
    row_a[t] = message
    got = exchange(row_a, t, nt, "tm", 0)
    eh = rows[...].astype(BF16)
    rest = rows[...] - eh.astype(F32)
    em = rest.astype(BF16)
    el = (rest - em.astype(F32)).astype(BF16)
    back = lax.dot_general(
        jnp.concatenate([x3[0 : 2 * D, :], eh, em, el, jnp.zeros((8, E), BF16)], axis=0),
        place[...],
        (((1,), (1,)), ((), ())),
        preferred_element_type=F32,
    )
    dir_o[...] = back[:D] + back[D : 2 * D]
    eta_o[...] = back[2 * D : 2 * D + 8] + back[2 * D + 8 : 2 * D + 16] + back[2 * D + 16 : 2 * D + 24]
    know("space", 3)
    got.wait()
    total = row_a[0]
    for d in range(1, nt):
        total = total + row_a[d]
    know("space", 4)
    row_b[p] = total
    exchange(row_b, p, ns, "space", 1).wait()
    total = row_b[0]
    for d in range(1, ns):
        total = total + row_b[d]
    tot_o[...] = total

    @pl.when(t < nt - 1)
    def _():
        arrived(end_in, end_send.at[0])
        arrived(edge_in, end_send.at[1])

    for side, there in ((0, p < ns - 1), (1, p > 0)):

        @pl.when(there)
        def _():
            arrived(rim_in.at[:, side], rim_send.at[side])

    arrived(row_b.at[pl.ds(0, nt + ns - 2)], sum_send.at[0])


def finish(count, init_v, dir_v, eta_v, tot_v, out_h, ind_h, est_h, out_v, ind_v, est_v, sem):
    cross, square, base, mixed, quad = (tot_v[0:1, k : k + 1] for k in range(5))
    step = cross / square
    copies = []

    def send(src, dst):
        copies.append(pltpu.make_async_copy(src, dst, sem.at[len(copies)]))
        copies[-1].start()

    for k in range(OUT_PARTS):
        part_rows = pl.ds(k * (D // OUT_PARTS), D // OUT_PARTS)
        out_v[part_rows] = init_v[part_rows] + step * dir_v[part_rows]
        send(out_v.at[part_rows], out_h.at[0, part_rows])
    eta_total = base + step * mixed + step * step * quad
    eta = eta_v[2:3] + step * eta_v[3:4] + step * step * eta_v[4:5]
    ind_v[...] = eta * count / eta_total
    send(ind_v, ind_h)
    est_v[...] = jnp.broadcast_to(jnp.sqrt(eta_total / count), (1, NB))
    send(est_v, est_h)
    for copy in copies:
        copy.wait()


def on_device(nt, ns, initial, rhs, coef, stiffness, block_inverse, face_proj, lift, time_lift, neighbour, boundary, send_list):
    vmem = pltpu.VMEM
    hbm_spec = pl.BlockSpec(memory_space=pltpu.HBM)
    vmem_spec = pl.BlockSpec(memory_space=vmem)
    dma = pltpu.SemaphoreType.DMA
    iterate, direction, eta, totals = pl.pallas_call(
        functools.partial(kernel, nt, ns),
        out_shape=(
            jax.ShapeDtypeStruct((D, E), F32),
            jax.ShapeDtypeStruct((D, E), F32),
            jax.ShapeDtypeStruct((8, E), F32),
            jax.ShapeDtypeStruct((1, NB), F32),
        ),
        in_specs=[hbm_spec] * 11,
        out_specs=[vmem_spec] * 4,
        scratch_shapes=[
            vmem((D, E), F32),
            vmem((1, E), F32),
            vmem((2 * D + 2 * R + H, D), F32),
            vmem((2, 6, E), jnp.int32),
            vmem((2, NB), jnp.int32),
            vmem((E, E), BF16),
            vmem((H, E), F32),
            vmem((2 * D + 16, E), BF16),
            vmem((3 * D, E), BF16),
            vmem((3 * H, E), BF16),
            vmem((R + D, E), F32),
            vmem((LAYERS * 2 * FD, 2 * NB), BF16),
            vmem((2, 256, E), F32),
            vmem((D, E), F32),
            vmem((D, E), F32),
            vmem((2, H, NB), F32),
            vmem((2, H, NB), F32),
            vmem((D, E), F32),
            vmem((D, E), F32),
            vmem((8, E), F32),
            vmem((R + D, 3 * D), BF16),
            vmem((D, 3 * R), BF16),
            vmem((D, 3 * H), BF16),
            vmem((D, 3 * D), BF16),
            vmem((D, 3 * H), BF16),
            vmem((2, 2 * D, 3 * FD), BF16),
            vmem((2, 2, FD, NB), F32),
            vmem((2, 2, FD, NB), F32),
            vmem((2, H, E), F32),
            vmem((nt, 1, NB), F32),
            vmem((nt + ns, 1, NB), F32),
            dma((6,)),
            dma((2,)),
            dma((6,)),
            dma((2,)),
            dma((2, 2)),
            dma((1,)),
            dma((2,)),
            pltpu.SemaphoreType.REGULAR((max(1, len(rounds(nt, TM_RADIUS)) + len(rounds(ns, SPACE_RADIUS))),)),
        ],
        compiler_params=pltpu.CompilerParams(collective_id=0, has_side_effects=True, vmem_limit_bytes=40 * 1024 * 1024),
        cost_estimate=pl.CostEstimate(flops=4 * 10**9, bytes_accessed=3 * 2**20, transcendentals=0),
    )(
        *(
            pltpu.with_memory_space_constraint(x, pltpu.HBM)
            for x in (
                initial,
                rhs,
                coef.reshape(1, E),
                stiffness,
                block_inverse,
                face_proj,
                lift.T,
                time_lift.T,
                neighbour,
                boundary,
                send_list.reshape(2, NB),
            )
        )
    )
    smoothed, indicator, estimate = pl.pallas_call(
        functools.partial(finish, float(E * nt * ns)),
        out_shape=(
            jax.ShapeDtypeStruct((1, D, E), F32),
            jax.ShapeDtypeStruct((1, E), F32),
            jax.ShapeDtypeStruct((1, NB), F32),
        ),
        in_specs=[vmem_spec] * 4,
        out_specs=[hbm_spec] * 3,
        scratch_shapes=[
            vmem((D, E), F32),
            vmem((1, E), F32),
            vmem((1, NB), F32),
            dma((OUT_PARTS + 2,)),
        ],
        compiler_params=pltpu.CompilerParams(vmem_limit_bytes=8 * 1024 * 1024),
        cost_estimate=pl.CostEstimate(flops=3 * 10**5, bytes_accessed=2**20, transcendentals=0),
    )(iterate, direction, eta, totals)
    return smoothed, indicator, estimate[0, :1]


def solution(mesh):
    return jax.shard_map(
        functools.partial(on_device, mesh.shape["tm"], mesh.shape["space"]),
        mesh=mesh,
        in_specs=(
            P("tm", None, "space"),
            P("tm", None, "space"),
            P("space"),
            P(),
            P(),
            P(),
            P(),
            P(),
            P(None, "space"),
            P(None, "space"),
            P("space"),
        ),
        out_specs=(P("tm", None, "space"), P("tm", "space"), P()),
        check_vma=False,
    )
```
